256 devices in a mesh: row: 32 (over z, x_lo, core), col: 8 (over x_hi, y).
Axes of the slice: x: 4 (x_hi: 2, x_lo: 2; x = x_hi * 2 + x_lo), y: 4, z: 8, core: 2. Of those that a mesh axis runs over, the one named last changes fastest.
Arguments:
- object_slices: float32 [2, 2, 3072, 768], P(None, None, 'row', 'col'), may hold values from -4 to 4
- probe: float32 [2, 192, 192], replicated, may hold values from -4 to 4
- propagator_phase: float32 [192, 192], replicated, may hold values from -3.140625 to 3.140625
- measured: float32 [32, 8, 2, 192, 192], P('row', 'col'), may hold values from 0 to 2
- offsets: int32 [32, 8, 2, 2], P('row', 'col'), may hold values from 0 to 95
- counts: int32 [32, 8], P('row', 'col'), may hold values from 1 to 2
Outputs:
- object_out: float32 [2, 2, 3072, 768], P(None, None, 'row', 'col')
- probe_out: float32 [2, 192, 192], replicated
The draws below stay inside these ranges and needn't reach their ends.
Inputs may be any that keep to these rules, and one draw needn't show every extreme that they name: The slots below counts hold the tile's scan positions; the others are unused.
All inputs are finite; a program needn't handle non-finite values.
Results may differ from the reference program's by a relative error of at most 0.00014.
Values sent between devices are 32-bit elements; how exact they have to be, the bound alone decides.
A program may use at most 64 MiB of HBM per device.

```python
import jax
import jax.numpy as jnp
from jax import lax

TILE = 96
PROBE_PIXELS = 192
SLOTS = 2
ITERS = 1
GRID_ROWS = 32
GRID_COLS = 8
NY = 3072
NX = 768


def set_ends(array, stream_key, least, largest):
    place = [jax.random.randint(jax.random.fold_in(stream_key, axis), (), 0, length) for axis, length in enumerate(array.shape)]
    longest = array.shape.index(max(array.shape))
    next_to = place[:longest] + [(place[longest] + 1) % array.shape[longest]] + place[longest + 1:]
    return array.at[tuple(place)].set(least).at[tuple(next_to)].set(largest)


def levels(stream_key, shape, split, least, largest):
    loudness = 1.0
    for position, shards_of in split:
        draws = jax.random.uniform(jax.random.fold_in(jax.random.fold_in(stream_key, 6), position), (shards_of,), jnp.float32, least / len(split), largest / len(split))
        loudness = loudness * jnp.repeat(jnp.exp(draws), shape[position] // shards_of).reshape((-1,) + (1,) * (len(shape) - 1 - position))
    return loudness


def gaussian(stream_key, dims, deviation, bound, split=(), kind=jnp.bfloat16):
    entries = jax.random.normal(stream_key, dims, jnp.float32) * deviation
    if len(split) > 0:
        entries = levels(stream_key, dims, split, -0.22, 0.18) * entries
    return jnp.clip(entries, min=-bound, max=bound).astype(kind)


def setup_inputs(seed: int = 0) -> dict:
    arg_keys = jax.random.split(jax.random.key(seed), 7)
    return {
        "object_slices": gaussian(arg_keys[0], (2, 2, NY, NX), 0.7, 4.0, ((2, 32), (3, 8)), jnp.float32),
        "probe": gaussian(arg_keys[1], (2, PROBE_PIXELS, PROBE_PIXELS), 0.7, 4.0, (), jnp.float32),
        "propagator_phase": jnp.clip(jax.random.uniform(arg_keys[2], (PROBE_PIXELS, PROBE_PIXELS), jnp.float32, -3.140625, 3.140625), -3.140625, 3.140625),
        "measured": jnp.clip(2.0 * jax.random.uniform(arg_keys[3], (GRID_ROWS, GRID_COLS, SLOTS, PROBE_PIXELS, PROBE_PIXELS), jnp.float32) ** levels(arg_keys[3], (GRID_ROWS, GRID_COLS, SLOTS, PROBE_PIXELS, PROBE_PIXELS), ((0, 32), (1, 8)), -0.2, 0.2), 0.0, 2.0),
        "offsets": set_ends(jax.random.randint(arg_keys[4], (GRID_ROWS, GRID_COLS, SLOTS, 2), 0, TILE), jax.random.fold_in(arg_keys[4], 1), 0, TILE - 1).astype(jnp.int32),
        "counts": set_ends(jax.random.randint(arg_keys[5], (GRID_ROWS, GRID_COLS), 1, SLOTS + 1), jax.random.fold_in(arg_keys[5], 1), 1, SLOTS).astype(jnp.int32),
    }


object_rate = 0.02
probe_rate = 0.3


def split_parts(value):
    return jnp.stack([jnp.real(value), jnp.imag(value)])


def position_contributions(object_window, incident_wave, slice_transmission, measured_intensity):
    first = lax.complex(object_window[0, 0], object_window[0, 1])
    second = lax.complex(object_window[1, 0], object_window[1, 1])
    entry = incident_wave * first
    carried = jnp.fft.ifft2(slice_transmission * jnp.fft.fft2(entry, norm="ortho"), norm="ortho")
    leaving = carried * second
    detector_field = jnp.fft.fft2(leaving, norm="ortho")
    model_intensity = jnp.real(detector_field) ** 2 + jnp.imag(detector_field) ** 2
    backward_wave = jnp.fft.ifft2((model_intensity - measured_intensity) * detector_field, norm="ortho")
    grad_second = jnp.conj(carried) * backward_wave
    before = jnp.conj(second) * backward_wave
    inner_wave = jnp.fft.ifft2(jnp.conj(slice_transmission) * jnp.fft.fft2(before, norm="ortho"), norm="ortho")
    grad_first = jnp.conj(incident_wave) * inner_wave
    grad_probe = jnp.conj(first) * inner_wave
    return jnp.stack([split_parts(grad_first), split_parts(grad_second)]), split_parts(grad_probe)


def reference(object_slices, probe, propagator_phase, measured, offsets, counts):
    slice_transmission = lax.complex(jnp.cos(propagator_phase), jnp.sin(propagator_phase))
    rows_count, cols_count = counts.shape
    slot_ids = jnp.arange(SLOTS, dtype=jnp.int32)
    tile_rows = jnp.arange(rows_count, dtype=jnp.int32)[:, None, None] * TILE
    tile_cols = jnp.arange(cols_count, dtype=jnp.int32)[None, :, None] * TILE
    row_offsets = (tile_rows + offsets[..., 0] + (TILE - PROBE_PIXELS // 2)).reshape(-1).astype(jnp.int32)
    column_offsets = (tile_cols + offsets[..., 1] + (TILE - PROBE_PIXELS // 2)).reshape(-1).astype(jnp.int32)
    position_weights = (slot_ids[None, None, :] < counts[:, :, None]).astype(object_slices.dtype).reshape(-1)
    measured_flat = measured.reshape(-1, PROBE_PIXELS, PROBE_PIXELS)
    current = object_slices
    wave = probe
    for iteration in range(ITERS):
        padded = jnp.pad(current, ((0, 0), (0, 0), (TILE, TILE), (TILE, TILE)))
        incident_wave = lax.complex(wave[0], wave[1])

        def accumulate_gradient(carry, scan_item):
            object_gradient, wave_gradient = carry
            row_offset, column_offset, position_weight, measured_intensity = scan_item
            zero = jnp.zeros((), jnp.int32)
            corner = (zero, zero, row_offset, column_offset)
            object_window = lax.dynamic_slice(padded, corner, (2, 2, PROBE_PIXELS, PROBE_PIXELS))
            object_contribution, wave_contribution = position_contributions(object_window, incident_wave, slice_transmission, measured_intensity)
            previous = lax.dynamic_slice(object_gradient, corner, (2, 2, PROBE_PIXELS, PROBE_PIXELS))
            object_gradient = lax.dynamic_update_slice(object_gradient, previous + position_weight * object_contribution, corner)
            return (object_gradient, wave_gradient + position_weight * wave_contribution), None

        window_corner = (jnp.zeros_like(padded), jnp.zeros_like(wave))
        (object_gradient, wave_gradient), ignored_value = lax.scan(accumulate_gradient, window_corner, (row_offsets, column_offsets, position_weights, measured_flat))
        current = current - object_rate * object_gradient[:, :, TILE:-TILE, TILE:-TILE]
        wave = wave - (probe_rate / (SLOTS * rows_count * cols_count)) * wave_gradient
    return current, wave
```

```python
import functools

import jax
import jax.numpy as jnp
import ml_dtypes
import numpy as np
from jax import lax
from jax.experimental import pallas as pl
from jax.experimental.pallas import tpu as pltpu
from jax.sharding import PartitionSpec as P

OBJECT_RATE = 0.02
PROBE_RATE = 0.3
TILE = 96
WIDTH = 192
LANES = 256
SLOTS = 2
HALF = 288
MESH = pl.DeviceIdType.MESH
AROUND = [(i, j) for i in (-1, 0, 1) for j in (-1, 0, 1) if (i, j) != (0, 0)]
F32 = jnp.float32
BF16 = jnp.bfloat16


def place(i, j):
    return (i + 1) * 3 + (j + 1)


def matrices():
    n = np.arange(WIDTH)
    angle = 2.0 * np.pi * (np.outer(n, n) % WIDTH) / WIDTH
    c = np.cos(angle) / np.sqrt(WIDTH)
    s = np.sin(angle) / np.sqrt(WIDTH)
    right = np.zeros((2 * LANES, 2 * LANES))
    right[:WIDTH, :WIDTH] = c
    right[:WIDTH, LANES : LANES + WIDTH] = -s
    right[LANES : LANES + WIDTH, :WIDTH] = s
    right[LANES : LANES + WIDTH, LANES : LANES + WIDTH] = c
    left = np.block([[c, s], [-s, c]])
    parts = []
    for full in (right, left):
        high = full.astype(np.float32).astype(ml_dtypes.bfloat16)
        low = (full - high.astype(np.float64)).astype(np.float32).astype(ml_dtypes.bfloat16)
        parts += [high, low]
    return parts


def two(x):
    high = x.astype(BF16)
    return high, (x - high.astype(F32)).astype(BF16)


def times(ar, ai, br, bi):
    return ar * br - ai * bi, ar * bi + ai * br


def times_conj(ar, ai, br, bi):
    return ar * br + ai * bi, ar * bi - ai * br


def dot(a, b):
    return jnp.dot(a, b, preferred_element_type=F32)


def chunks(body, step, total=WIDTH):
    def run(i, carry):
        body(pl.multiple_of(i * step, step))
        return carry

    lax.fori_loop(0, total // step, run, 0)


def kernel(
    rows, cols, share, owners,
    offsets, counts, obj, probe, phase, measured, wrh, wrl, wlh, wll,
    obj_out, probe_out,
    own, halo, band, win, wave, trans, xh, xl, lh, ll, y, carried, shift,
    gsend, grecv, pack, half_in, plane_in, deep_in, total,
    halo_s, halo_r, grad_s, grad_r, pair_s, pair_r, plane_s, plane_r, deep_s, deep_r,
    back_s, back_r, last_s, last_r,
):
    r = lax.axis_index("row")
    c = lax.axis_index("col")
    core = lax.rem(r, 2)
    x_lo = lax.rem(lax.div(r, 2), 2)
    z = lax.div(r, 4)
    depth = rows // 4
    group = 2 * cols
    me = x_lo * cols + c
    other = (r + 1 - 2 * core, c)

    def beside(i, j):
        return (lax.rem(r + i + rows, rows), lax.rem(c + j + cols, cols))

    def in_plane(p):
        return (z * 4 + (p // cols) * 2 + core, p % cols)

    def in_depth(k):
        return (k * 4 + x_lo * 2 + core, c)

    def inside(i, j):
        return (r + i >= 0) & (r + i < rows) & (c + j >= 0) & (c + j < cols)

    barrier = pltpu.get_barrier_semaphore()

    def greet(device):
        pl.semaphore_signal(barrier, inc=1, device_id=device, device_id_type=MESH)

    for i, j in AROUND:
        greet(beside(i, j))
    greet(other)
    for d in range(1, group):
        p = lax.rem(me + d, group)
        greet((z * 4 + lax.div(p, cols) * 2 + core, lax.rem(p, cols)))
    for d in range(1, depth):
        greet((lax.rem(z + d, depth) * 4 + x_lo * 2 + core, c))

    for s in range(2):
        for k in range(2):
            own[s, k] = jnp.zeros((TILE, 128), F32)
            own[s, k, :, :TILE] = obj[s, k]

    pl.semaphore_wait(barrier, len(AROUND) + group + depth - 1)

    def halo_copy(s, i, j):
        return pltpu.make_async_remote_copy(
            src_ref=own.at[s],
            dst_ref=halo.at[s, place(-i, -j)],
            send_sem=halo_s.at[s, place(i, j)],
            recv_sem=halo_r.at[s, place(-i, -j)],
            device_id=beside(i, j),
            device_id_type=MESH,
        )

    def grad_copy(s, i, j):
        return pltpu.make_async_remote_copy(
            src_ref=gsend.at[s, place(i, j)],
            dst_ref=grecv.at[s, place(-i, -j)],
            send_sem=grad_s.at[s, place(i, j)],
            recv_sem=grad_r.at[s, place(-i, -j)],
            device_id=beside(i, j),
            device_id_type=MESH,
        )

    for s in range(2):
        for i, j in AROUND:
            halo_copy(s, i, j).start()

    for k in range(2):
        wave[k] = jnp.zeros((WIDTH, LANES), F32)
        wave[k, :, :WIDTH] = probe[k]
        trans[k] = jnp.zeros((WIDTH, LANES), F32)
    trans[0, :, :WIDTH] = jnp.cos(phase[...])
    trans[1, :, :WIDTH] = jnp.sin(phase[...])
    for slot in range(SLOTS):
        for k in range(2):
            for m in range(2):
                shift[slot, k, m, :TILE] = jnp.zeros((TILE, 128), F32)
                shift[slot, k, m, TILE + WIDTH :] = jnp.zeros((TILE, 128), F32)

    ro = [offsets[0, 0, slot, 0] for slot in range(SLOTS)]
    co = [offsets[0, 0, slot, 1] for slot in range(SLOTS)]
    live = [slot < counts[0, 0] for slot in range(SLOTS)]

    def windows(s):
        for i in (-1, 0, 1):
            for k in range(2):
                pieces = []
                for j in (-1, 0, 1):
                    if (i, j) == (0, 0):
                        pieces.append(own[s, k])
                    else:
                        pieces.append(jnp.where(inside(i, j), halo[s, place(i, j), k], 0.0))
                lane = lax.broadcasted_iota(jnp.int32, (TILE, 128), 1)
                a = pieces[0]
                b = pltpu.roll(pieces[1], 96, 1)
                d = pltpu.roll(pieces[2], 64, 1)
                at = pl.ds((i + 1) * TILE, TILE)
                band[k, 0, at] = jnp.where(lane < 96, a, b)
                band[k, 1, at] = jnp.where(lane < 64, b, d)
                band[k, 2, at] = jnp.where(lane < 64, d, 0.0)
        for slot in range(SLOTS):
            for k in range(2):
                lane = lax.broadcasted_iota(jnp.int32, (WIDTH, 128), 1)
                turn = lax.rem(128 - co[slot], 128)
                at = pl.ds(ro[slot], WIDTH)
                v = [pltpu.roll(band[k, m, at], turn, 1) for m in range(3)]
                keep = lane < 128 - co[slot]
                win[s, slot, k, :, 0:128] = jnp.where(keep, v[0], v[1])
                win[s, slot, k, :, 128:256] = jnp.where(keep, v[1], v[2])

    def put(slot, at, step, re, im, inverse):
        if inverse:
            re, im = im, re
        to = pl.ds(slot * WIDTH + at, step)
        xh[to, :LANES], xl[to, :LANES] = two(re)
        xh[to, LANES:], xl[to, LANES:] = two(im)

    def transform():
        acc = dot(xh[...], wrh[...]) + dot(xl[...], wrh[...]) + dot(xh[...], wrl[...])
        for slot in range(SLOTS):
            part = acc[slot * WIDTH : (slot + 1) * WIDTH]
            lh[slot, :WIDTH], ll[slot, :WIDTH] = two(part[:, :LANES])
            lh[slot, WIDTH:], ll[slot, WIDTH:] = two(part[:, LANES:])
        for slot in range(SLOTS):
            y[slot] = (
                dot(wlh[...], lh[slot]) + dot(wlh[...], ll[slot]) + dot(wll[...], lh[slot])
            )

    def got(slot, at, step, inverse):
        one = y[slot, pl.ds(at, step), :]
        two_ = y[slot, pl.ds(WIDTH + at, step), :]
        return (two_, one) if inverse else (one, two_)

    step = 32

    def each(body):
        for slot in range(SLOTS):
            chunks(functools.partial(body, slot), step)

    def spread(s):
        for i in (-1, 0, 1):
            for k in range(2):
                lane = lax.broadcasted_iota(jnp.int32, (TILE, 128), 1)
                v = [0.0, 0.0, 0.0]
                for slot in range(SLOTS):
                    at = pl.ds(TILE * (i + 2) - ro[slot], TILE)
                    a = pltpu.roll(shift[slot, k, 0, at], co[slot], 1)
                    b = pltpu.roll(shift[slot, k, 1, at], co[slot], 1)
                    wrap = lane < co[slot]
                    v[0] = v[0] + jnp.where(wrap, 0.0, a)
                    v[1] = v[1] + jnp.where(wrap, a, b)
                    v[2] = v[2] + jnp.where(wrap, b, 0.0)
                gsend[s, place(i, -1), k] = v[0]
                gsend[s, place(i, 0), k] = jnp.where(
                    lane < 32, pltpu.roll(v[0], 32, 1), pltpu.roll(v[1], 32, 1)
                )
                gsend[s, place(i, 1), k] = jnp.where(
                    lane < 64, pltpu.roll(v[1], 64, 1), pltpu.roll(v[2], 64, 1)
                )

    def shifted(slot, at, re, im):
        to = pl.ds(TILE + at, step)
        for k, part in enumerate((re, im)):
            part = jnp.where(live[slot], part, 0.0)
            shift[slot, k, 0, to] = part[:, :128]
            shift[slot, k, 1, to] = part[:, 128:]

    for i, j in AROUND:
        halo_copy(0, i, j).wait_recv()
    windows(0)

    def enter(slot, at):
        d = pl.ds(at, step)
        re, im = times(wave[0, d], wave[1, d], win[0, slot, 0, d], win[0, slot, 1, d])
        put(slot, at, step, re, im, False)

    each(enter)
    transform()

    def carry(slot, at):
        d = pl.ds(at, step)
        re, im = got(slot, at, step, False)
        re, im = times(trans[0, d], trans[1, d], re, im)
        put(slot, at, step, re, im, True)

    each(carry)
    transform()

    for i, j in AROUND:
        halo_copy(1, i, j).wait_recv()
    windows(1)

    def leave(slot, at):
        d = pl.ds(at, step)
        re, im = got(slot, at, step, True)
        carried[slot, 0, d] = re
        carried[slot, 1, d] = im
        re, im = times(re, im, win[1, slot, 0, d], win[1, slot, 1, d])
        put(slot, at, step, re, im, False)

    each(leave)
    transform()

    def residual(slot, at):
        re, im = got(slot, at, step, False)
        seen = jnp.concatenate(
            [measured[slot, pl.ds(at, step), :], jnp.zeros((step, LANES - WIDTH), F32)], axis=1
        )
        resid = re * re + im * im - seen
        put(slot, at, step, resid * re, resid * im, True)

    each(residual)
    transform()

    def second(slot, at):
        d = pl.ds(at, step)
        re, im = got(slot, at, step, True)
        shifted(slot, at, *times_conj(carried[slot, 0, d], carried[slot, 1, d], re, im))
        re, im = times_conj(win[1, slot, 0, d], win[1, slot, 1, d], re, im)
        put(slot, at, step, re, im, False)

    each(second)
    spread(1)
    for i, j in AROUND:
        grad_copy(1, i, j).start()
    transform()

    def inner(slot, at):
        d = pl.ds(at, step)
        re, im = got(slot, at, step, False)
        re, im = times_conj(trans[0, d], trans[1, d], re, im)
        put(slot, at, step, re, im, True)

    each(inner)
    transform()

    def probe_part(at):
        d = pl.ds(at, step)
        re = jnp.zeros((step, LANES), F32)
        im = jnp.zeros((step, LANES), F32)
        for slot in range(SLOTS):
            ir, ii = got(slot, at, step, True)
            pr, pi = times_conj(win[0, slot, 0, d], win[0, slot, 1, d], ir, ii)
            re = re + jnp.where(live[slot], pr, 0.0)
            im = im + jnp.where(live[slot], pi, 0.0)
            shifted(slot, at, *times_conj(wave[0, d], wave[1, d], ir, ii))
        lane = lax.broadcasted_iota(jnp.int32, (step, 128), 1)
        pack[d] = re[:, :128]
        pack[pl.ds(WIDTH + at, step)] = im[:, :128]
        pack[pl.ds(2 * WIDTH + at, step)] = jnp.where(
            lane < 64, re[:, 128:], pltpu.roll(im[:, 128:], 64, 1)
        )

    chunks(probe_part, step)

    mine = pl.multiple_of(HALF * core, 8)
    theirs = pl.multiple_of(HALF * (1 - core), 8)
    pair = pltpu.make_async_remote_copy(
        src_ref=pack.at[pl.ds(theirs, HALF)],
        dst_ref=half_in,
        send_sem=pair_s,
        recv_sem=pair_r,
        device_id=other,
        device_id_type=MESH,
    )
    pair.start()

    spread(0)
    for i, j in AROUND:
        grad_copy(0, i, j).start()

    pair.wait_recv()
    half_in[...] = half_in[...] + pack[pl.ds(mine, HALF)]

    def plane_copy(q, sender):
        return pltpu.make_async_remote_copy(
            src_ref=half_in.at[pl.ds(q * share, share)],
            dst_ref=plane_in.at[sender],
            send_sem=plane_s.at[q],
            recv_sem=plane_r.at[sender],
            device_id=in_plane(q),
            device_id_type=MESH,
        )

    for q in range(owners):
        @pl.when(me != q)
        def _():
            plane_copy(q, me).start()

    for i, j in AROUND:
        grad_copy(1, i, j).wait_recv()

    def update(s):
        for k in range(2):
            whole = gsend[s, place(0, 0), k]
            for i, j in AROUND:
                whole = whole + jnp.where(inside(i, j), grecv[s, place(i, j), k], 0.0)
            obj_out[s, k] = obj[s, k] - OBJECT_RATE * whole[:, :TILE]

    update(1)

    my_share = pl.multiple_of(me * share, 8)

    def deep_copy(k, sender):
        return pltpu.make_async_remote_copy(
            src_ref=deep_in.at[z],
            dst_ref=deep_in.at[sender],
            send_sem=deep_s.at[k],
            recv_sem=deep_r.at[sender],
            device_id=in_depth(k),
            device_id_type=MESH,
        )

    @pl.when(me < owners)
    def _():
        whole = half_in[pl.ds(my_share, share)]
        for p in range(group):
            @pl.when(me != p)
            def _():
                plane_copy(0, p).wait_recv()
        plane_in[me] = whole
        whole = plane_in[0]
        for p in range(1, group):
            whole = whole + plane_in[p]
        deep_in[z] = whole
        for k in range(depth):
            @pl.when(z != k)
            def _():
                deep_copy(k, z).start()

    for i, j in AROUND:
        grad_copy(0, i, j).wait_recv()
    update(0)

    def back_copy(p, sender):
        at = pl.ds(pl.multiple_of(mine + sender * share, 8), share)
        return pltpu.make_async_remote_copy(
            src_ref=total.at[at],
            dst_ref=total.at[at],
            send_sem=back_s.at[p],
            recv_sem=back_r.at[sender],
            device_id=in_plane(p),
            device_id_type=MESH,
        )

    def last_copy(base, q):
        at = pl.ds(pl.multiple_of(base + q * share, 8), share)
        return pltpu.make_async_remote_copy(
            src_ref=total.at[at],
            dst_ref=total.at[at],
            send_sem=last_s.at[q],
            recv_sem=last_r.at[q],
            device_id=other,
            device_id_type=MESH,
        )

    @pl.when(me < owners)
    def _():
        for k in range(depth):
            @pl.when(z != k)
            def _():
                deep_copy(0, k).wait_recv()
        whole = deep_in[0]
        for k in range(1, depth):
            whole = whole + deep_in[k]
        total[pl.ds(pl.multiple_of(mine + my_share, 8), share)] = whole
        for p in range(group):
            @pl.when(me != p)
            def _():
                back_copy(p, me).start()

    for q in range(owners):
        @pl.when(me != q)
        def _():
            back_copy(0, q).wait_recv()
        last_copy(mine, q).start()
    for q in range(owners):
        last_copy(theirs, q).wait_recv()

    rate = PROBE_RATE / (SLOTS * rows * cols)

    def finish(at):
        d = pl.ds(at, step)
        re = total[d]
        im = total[pl.ds(WIDTH + at, step)]
        rest = total[pl.ds(2 * WIDTH + at, step)]
        probe_out[0, d, :128] = probe[0, d, :128] - rate * re
        probe_out[1, d, :128] = probe[1, d, :128] - rate * im
        probe_out[0, d, 128:] = probe[0, d, 128:] - rate * rest[:, :64]
        probe_out[1, d, 128:] = probe[1, d, 128:] - rate * pltpu.roll(rest, 64, 1)[:, :64]

    chunks(finish, step)

    for s in range(2):
        for i, j in AROUND:
            halo_copy(s, i, j).wait_send()
            grad_copy(s, i, j).wait_send()
    pair.wait_send()
    for q in range(owners):
        @pl.when(me != q)
        def _():
            plane_copy(q, me).wait_send()
        last_copy(mine, q).wait_send()

    @pl.when(me < owners)
    def _():
        for k in range(depth):
            @pl.when(z != k)
            def _():
                deep_copy(k, z).wait_send()
        for p in range(group):
            @pl.when(me != p)
            def _():
                back_copy(p, me).wait_send()


def solution(mesh):
    rows, cols = mesh.shape["row"], mesh.shape["col"]
    group, depth = 2 * cols, rows // 4
    share = -(-(HALF // 8) // group) * 8
    owners = HALF // share
    consts = matrices()

    def shards(object_slices, probe, propagator_phase, measured, offsets, counts):
        vmem = pl.BlockSpec(memory_space=pltpu.VMEM)
        smem = pl.BlockSpec(memory_space=pltpu.SMEM)
        dma = pltpu.SemaphoreType.DMA
        square = (WIDTH, LANES)
        return pl.pallas_call(
            functools.partial(kernel, rows, cols, share, owners),
            out_shape=(
                jax.ShapeDtypeStruct(object_slices.shape, F32),
                jax.ShapeDtypeStruct(probe.shape, F32),
            ),
            in_specs=[smem, smem] + [vmem] * 8,
            out_specs=(vmem, vmem),
            scratch_shapes=[
                pltpu.VMEM((2, 2, TILE, 128), F32),
                pltpu.VMEM((2, 9, 2, TILE, 128), F32),
                pltpu.VMEM((2, 3, 3 * TILE, 128), F32),
                pltpu.VMEM((2, SLOTS, 2) + square, F32),
                pltpu.VMEM((2,) + square, F32),
                pltpu.VMEM((2,) + square, F32),
                pltpu.VMEM((SLOTS * WIDTH, 2 * LANES), BF16),
                pltpu.VMEM((SLOTS * WIDTH, 2 * LANES), BF16),
                pltpu.VMEM((SLOTS, 2 * WIDTH, LANES), BF16),
                pltpu.VMEM((SLOTS, 2 * WIDTH, LANES), BF16),
                pltpu.VMEM((SLOTS, 2 * WIDTH, LANES), F32),
                pltpu.VMEM((SLOTS, 2) + square, F32),
                pltpu.VMEM((SLOTS, 2, 2, 4 * TILE, 128), F32),
                pltpu.VMEM((2, 9, 2, TILE, 128), F32),
                pltpu.VMEM((2, 9, 2, TILE, 128), F32),
                pltpu.VMEM((2 * HALF, 128), F32),
                pltpu.VMEM((HALF, 128), F32),
                pltpu.VMEM((group, share, 128), F32),
                pltpu.VMEM((depth, share, 128), F32),
                pltpu.VMEM((2 * HALF, 128), F32),
                dma((2, 9)), dma((2, 9)), dma((2, 9)), dma((2, 9)),
                dma, dma,
                dma((owners,)), dma((group,)),
                dma((depth,)), dma((depth,)),
                dma((group,)), dma((owners,)),
                dma((owners,)), dma((owners,)),
            ],
            compiler_params=pltpu.CompilerParams(
                collective_id=0, has_side_effects=True, vmem_limit_bytes=48 * 1024 * 1024
            ),
        )(
            offsets, counts, object_slices, probe, propagator_phase, measured[0, 0],
            *[jnp.asarray(m) for m in consts],
        )

    return jax.shard_map(
        shards,
        mesh=mesh,
        in_specs=(
            P(None, None, "row", "col"),
            P(),
            P(),
            P("row", "col", None, None, None),
            P("row", "col", None, None),
            P("row", "col"),
        ),
        out_specs=(P(None, None, "row", "col"), P()),
        check_vma=False,
    )
```

```python
import functools

import jax
import jax.numpy as jnp
import ml_dtypes
import numpy as np
from jax import lax
from jax.experimental import pallas as pl
from jax.experimental.pallas import tpu as pltpu
from jax.sharding import PartitionSpec as P

OBJECT_RATE = 0.02
PROBE_RATE = 0.3
TILE = 96
WIDTH = 192
LANES = 256
SLOTS = 2
HALF = 288
PART = 48
MESH = pl.DeviceIdType.MESH
AROUND = [(i, j) for i in (-1, 0, 1) for j in (-1, 0, 1) if (i, j) != (0, 0)]
F32 = jnp.float32
BF16 = jnp.bfloat16


def place(i, j):
    return (i + 1) * 3 + (j + 1)


def matrices():
    n = np.arange(WIDTH)
    angle = 2.0 * np.pi * (np.outer(n, n) % WIDTH) / WIDTH
    c = np.cos(angle) / np.sqrt(WIDTH)
    s = np.sin(angle) / np.sqrt(WIDTH)
    right = np.zeros((2 * LANES, 2 * LANES))
    right[:WIDTH, :WIDTH] = c
    right[:WIDTH, LANES : LANES + WIDTH] = -s
    right[LANES : LANES + WIDTH, :WIDTH] = s
    right[LANES : LANES + WIDTH, LANES : LANES + WIDTH] = c
    left = np.block([[c, s], [-s, c]])
    parts = []
    for full in (right, left):
        high = full.astype(np.float32).astype(ml_dtypes.bfloat16)
        low = (full - high.astype(np.float64)).astype(np.float32).astype(ml_dtypes.bfloat16)
        parts += [high, low]
    return parts


def two(x):
    high = x.astype(BF16)
    return high, (x - high.astype(F32)).astype(BF16)


def times(ar, ai, br, bi):
    return ar * br - ai * bi, ar * bi + ai * br


def times_conj(ar, ai, br, bi):
    return ar * br + ai * bi, ar * bi - ai * br


def packed(a, b, c, d):
    lane = lax.broadcasted_iota(jnp.int32, a.shape, 1)
    b, c, d = pltpu.roll(b, 96, 1), pltpu.roll(c, 64, 1), pltpu.roll(d, 32, 1)
    return jnp.where(lane < 96, a, b), jnp.where(lane < 64, b, c), jnp.where(lane < 32, c, d)


def unpacked(u, v, w):
    lane = lax.broadcasted_iota(jnp.int32, u.shape, 1)
    b = jnp.where(lane < 32, pltpu.roll(u, 32, 1), pltpu.roll(v, 32, 1))
    c = jnp.where(lane < 64, pltpu.roll(v, 64, 1), pltpu.roll(w, 64, 1))
    return u, b, c, pltpu.roll(w, 96, 1)


def dot(a, b):
    return jnp.dot(a, b, preferred_element_type=F32)


def chunks(body, step, total=WIDTH):
    for at in range(0, total, step):
        body(at)


def kernel(
    rows, cols, share, owners,
    offsets_in, counts_in, obj_in, probe_in, phase_in, measured_in, *rest,
):
    wide_in, (obj_out, probe_out), rest = rest[:4], rest[4:6], rest[6:]
    fetch(rows, cols, share, owners, offsets_in, counts_in, obj_in, probe_in, phase_in,
          measured_in, wide_in, obj_out, probe_out, *rest)


def fetch(
    rows, cols, share, owners,
    offsets_in, counts_in, obj_in, probe_in, phase_in, measured_in, wide_in,
    obj_out, probe_out,
    offsets, counts, obj, probe, phase, measured, wrh, wrl, wlh, wll, load,
    wide, own, halo, band, win, wave, trans, xh, xl, lh, ll, y, carried, shift,
    gsend, grecv, pack, half_in, plane_in, deep_in, total,
    halo_s, halo_r, grad_s, grad_r, pair_s, pair_r, plane_s, plane_r, deep_s, deep_r,
    back_s, back_r, last_s, last_r,
):
    r = lax.axis_index("row")
    c = lax.axis_index("col")
    core = lax.rem(r, 2)
    x_lo = lax.rem(lax.div(r, 2), 2)
    z = lax.div(r, 4)
    depth = rows // 4
    group = 2 * cols
    me = x_lo * cols + c
    other = (r + 1 - 2 * core, c)

    def beside(i, j):
        return (lax.rem(r + i + rows, rows), lax.rem(c + j + cols, cols))

    def in_plane(p):
        return (z * 4 + (p // cols) * 2 + core, p % cols)

    def in_depth(k):
        return (k * 4 + x_lo * 2 + core, c)

    def inside(i, j):
        return (r + i >= 0) & (r + i < rows) & (c + j >= 0) & (c + j < cols)

    loads = [
        pltpu.make_async_copy(a, b, load.at[i])
        for i, (a, b) in enumerate(
            zip(
                (obj_in, offsets_in, counts_in, probe_in, phase_in, *wide_in, measured_in.at[0, 0]),
                (obj, offsets, counts, probe, phase, wrh, wrl, wlh, wll, measured),
            )
        )
    ]
    for one in loads:
        one.start()

    barrier = pltpu.get_barrier_semaphore()

    def greet(device):
        pl.semaphore_signal(barrier, inc=1, device_id=device, device_id_type=MESH)

    for i, j in AROUND:
        greet(beside(i, j))
    greet(other)
    for d in range(1, group):
        p = lax.rem(me + d, group)
        greet((z * 4 + lax.div(p, cols) * 2 + core, lax.rem(p, cols)))
    for d in range(1, depth):
        greet((lax.rem(z + d, depth) * 4 + x_lo * 2 + core, c))

    loads[0].wait()
    for s in range(2):
        quarters = []
        for k in range(2):
            wide[s, k] = jnp.zeros((TILE, 128), F32)
            wide[s, k, :, :TILE] = obj[s, k]
            quarters += [wide[s, k, :PART], wide[s, k, PART:]]
        for m, v in enumerate(packed(*quarters)):
            own[s, m] = v

    pl.semaphore_wait(barrier, len(AROUND) + group + depth - 1)

    def halo_copy(s, i, j):
        return pltpu.make_async_remote_copy(
            src_ref=own.at[s],
            dst_ref=halo.at[s, place(-i, -j)],
            send_sem=halo_s.at[s, place(i, j)],
            recv_sem=halo_r.at[s, place(-i, -j)],
            device_id=beside(i, j),
            device_id_type=MESH,
        )

    def grad_copy(s, i, j):
        return pltpu.make_async_remote_copy(
            src_ref=gsend.at[s, place(i, j)],
            dst_ref=grecv.at[s, place(-i, -j)],
            send_sem=grad_s.at[s, place(i, j)],
            recv_sem=grad_r.at[s, place(-i, -j)],
            device_id=beside(i, j),
            device_id_type=MESH,
        )

    for s in range(2):
        for i, j in AROUND:
            halo_copy(s, i, j).start()

    for one in loads[1:]:
        one.wait()
    for k in range(2):
        wave[k] = jnp.zeros((WIDTH, LANES), F32)
        wave[k, :, :WIDTH] = probe[k]
        trans[k] = jnp.zeros((WIDTH, LANES), F32)
    trans[0, :, :WIDTH] = jnp.cos(phase[...])
    trans[1, :, :WIDTH] = jnp.sin(phase[...])
    for slot in range(SLOTS):
        for k in range(2):
            for m in range(2):
                shift[slot, k, m, :TILE] = jnp.zeros((TILE, 128), F32)
                shift[slot, k, m, TILE + WIDTH :] = jnp.zeros((TILE, 128), F32)

    ro = [offsets[0, 0, slot, 0] for slot in range(SLOTS)]
    co = [offsets[0, 0, slot, 1] for slot in range(SLOTS)]
    live = [slot < counts[0, 0] for slot in range(SLOTS)]

    def windows(s):
        lane = lax.broadcasted_iota(jnp.int32, (PART, 128), 1)
        for i in (-1, 0, 1):
            tiles = []
            for j in (-1, 0, 1):
                if (i, j) == (0, 0):
                    tiles.append(unpacked(*[own[s, m] for m in range(3)]))
                else:
                    keep = inside(i, j)
                    tiles.append(
                        unpacked(
                            *[jnp.where(keep, halo[s, place(i, j), m], 0.0) for m in range(3)]
                        )
                    )
            for k in range(2):
                for h in range(2):
                    a, b, d = [tile[2 * k + h] for tile in tiles]
                    b = pltpu.roll(b, 96, 1)
                    d = pltpu.roll(d, 64, 1)
                    at = pl.ds((i + 1) * TILE + h * PART, PART)
                    band[k, 0, at] = jnp.where(lane < 96, a, b)
                    band[k, 1, at] = jnp.where(lane < 64, b, d)
                    band[k, 2, at] = jnp.where(lane < 64, d, 0.0)
        for slot in range(SLOTS):
            for k in range(2):
                lane = lax.broadcasted_iota(jnp.int32, (WIDTH, 128), 1)
                turn = lax.rem(128 - co[slot], 128)
                at = pl.ds(ro[slot], WIDTH)
                v = [pltpu.roll(band[k, m, at], turn, 1) for m in range(3)]
                keep = lane < 128 - co[slot]
                win[s, slot, k, :, 0:128] = jnp.where(keep, v[0], v[1])
                win[s, slot, k, :, 128:256] = jnp.where(keep, v[1], v[2])

    def put(slot, at, step, re, im, inverse):
        if inverse:
            re, im = im, re
        to = pl.ds(slot * WIDTH + at, step)
        xh[to, :LANES], xl[to, :LANES] = two(re)
        xh[to, LANES:], xl[to, LANES:] = two(im)

    def transform():
        acc = dot(xh[...], wrh[...]) + dot(xl[...], wrh[...]) + dot(xh[...], wrl[...])
        for slot in range(SLOTS):
            part = acc[slot * WIDTH : (slot + 1) * WIDTH]
            lh[slot, :WIDTH], ll[slot, :WIDTH] = two(part[:, :LANES])
            lh[slot, WIDTH:], ll[slot, WIDTH:] = two(part[:, LANES:])
        for slot in range(SLOTS):
            y[slot] = (
                dot(wlh[...], lh[slot]) + dot(wlh[...], ll[slot]) + dot(wll[...], lh[slot])
            )

    def got(slot, at, step, inverse):
        one = y[slot, pl.ds(at, step), :]
        two_ = y[slot, pl.ds(WIDTH + at, step), :]
        return (two_, one) if inverse else (one, two_)

    step = 32

    def each(body):
        for slot in range(SLOTS):
            chunks(functools.partial(body, slot), step)

    def spread(s):
        lane = lax.broadcasted_iota(jnp.int32, (PART, 128), 1)
        for i in (-1, 0, 1):
            tiles = ([], [], [])
            for k in range(2):
                for h in range(2):
                    v = [0.0, 0.0, 0.0]
                    for slot in range(SLOTS):
                        at = pl.ds(TILE * (i + 2) + PART * h - ro[slot], PART)
                        a = pltpu.roll(shift[slot, k, 0, at], co[slot], 1)
                        b = pltpu.roll(shift[slot, k, 1, at], co[slot], 1)
                        wrap = lane < co[slot]
                        v[0] = v[0] + jnp.where(wrap, 0.0, a)
                        v[1] = v[1] + jnp.where(wrap, a, b)
                        v[2] = v[2] + jnp.where(wrap, b, 0.0)
                    tiles[0].append(v[0])
                    tiles[1].append(
                        jnp.where(lane < 32, pltpu.roll(v[0], 32, 1), pltpu.roll(v[1], 32, 1))
                    )
                    tiles[2].append(
                        jnp.where(lane < 64, pltpu.roll(v[1], 64, 1), pltpu.roll(v[2], 64, 1))
                    )
            for j in (-1, 0, 1):
                for m, part in enumerate(packed(*tiles[j + 1])):
                    gsend[s, place(i, j), m] = part

    def shifted(slot, at, re, im):
        to = pl.ds(TILE + at, step)
        for k, part in enumerate((re, im)):
            part = jnp.where(live[slot], part, 0.0)
            shift[slot, k, 0, to] = part[:, :128]
            shift[slot, k, 1, to] = part[:, 128:]

    for i, j in AROUND:
        halo_copy(0, i, j).wait_recv()
    windows(0)

    def enter(slot, at):
        d = pl.ds(at, step)
        re, im = times(wave[0, d], wave[1, d], win[0, slot, 0, d], win[0, slot, 1, d])
        put(slot, at, step, re, im, False)

    each(enter)
    transform()

    def carry(slot, at):
        d = pl.ds(at, step)
        re, im = got(slot, at, step, False)
        re, im = times(trans[0, d], trans[1, d], re, im)
        put(slot, at, step, re, im, True)

    each(carry)
    transform()

    for i, j in AROUND:
        halo_copy(1, i, j).wait_recv()
    windows(1)

    def leave(slot, at):
        d = pl.ds(at, step)
        re, im = got(slot, at, step, True)
        carried[slot, 0, d] = re
        carried[slot, 1, d] = im
        re, im = times(re, im, win[1, slot, 0, d], win[1, slot, 1, d])
        put(slot, at, step, re, im, False)

    each(leave)
    transform()

    def residual(slot, at):
        re, im = got(slot, at, step, False)
        seen = jnp.concatenate(
            [measured[slot, pl.ds(at, step), :], jnp.zeros((step, LANES - WIDTH), F32)], axis=1
        )
        resid = re * re + im * im - seen
        put(slot, at, step, resid * re, resid * im, True)

    each(residual)
    transform()

    def second(slot, at):
        d = pl.ds(at, step)
        re, im = got(slot, at, step, True)
        shifted(slot, at, *times_conj(carried[slot, 0, d], carried[slot, 1, d], re, im))
        re, im = times_conj(win[1, slot, 0, d], win[1, slot, 1, d], re, im)
        put(slot, at, step, re, im, False)

    each(second)
    spread(1)
    for i, j in AROUND:
        grad_copy(1, i, j).start()
    transform()

    def inner(slot, at):
        d = pl.ds(at, step)
        re, im = got(slot, at, step, False)
        re, im = times_conj(trans[0, d], trans[1, d], re, im)
        put(slot, at, step, re, im, True)

    each(inner)
    transform()

    def probe_part(at):
        d = pl.ds(at, step)
        re = jnp.zeros((step, LANES), F32)
        im = jnp.zeros((step, LANES), F32)
        for slot in range(SLOTS):
            ir, ii = got(slot, at, step, True)
            pr, pi = times_conj(win[0, slot, 0, d], win[0, slot, 1, d], ir, ii)
            re = re + jnp.where(live[slot], pr, 0.0)
            im = im + jnp.where(live[slot], pi, 0.0)
            shifted(slot, at, *times_conj(wave[0, d], wave[1, d], ir, ii))
        lane = lax.broadcasted_iota(jnp.int32, (step, 128), 1)
        pack[d] = re[:, :128]
        pack[pl.ds(WIDTH + at, step)] = im[:, :128]
        pack[pl.ds(2 * WIDTH + at, step)] = jnp.where(
            lane < 64, re[:, 128:], pltpu.roll(im[:, 128:], 64, 1)
        )

    chunks(probe_part, step)

    mine = pl.multiple_of(HALF * core, 8)
    theirs = pl.multiple_of(HALF * (1 - core), 8)
    pair = pltpu.make_async_remote_copy(
        src_ref=pack.at[pl.ds(theirs, HALF)],
        dst_ref=half_in,
        send_sem=pair_s,
        recv_sem=pair_r,
        device_id=other,
        device_id_type=MESH,
    )
    pair.start()

    spread(0)
    for i, j in AROUND:
        grad_copy(0, i, j).start()

    pair.wait_recv()
    half_in[...] = half_in[...] + pack[pl.ds(mine, HALF)]

    def plane_copy(q, sender):
        return pltpu.make_async_remote_copy(
            src_ref=half_in.at[pl.ds(q * share, share)],
            dst_ref=plane_in.at[sender],
            send_sem=plane_s.at[q],
            recv_sem=plane_r.at[sender],
            device_id=in_plane(q),
            device_id_type=MESH,
        )

    for q in range(owners):
        @pl.when(me != q)
        def _():
            plane_copy(q, me).start()

    for i, j in AROUND:
        grad_copy(1, i, j).wait_recv()

    def update(s):
        sums = []
        for m in range(3):
            whole = gsend[s, place(0, 0), m]
            for i, j in AROUND:
                whole = whole + jnp.where(inside(i, j), grecv[s, place(i, j), m], 0.0)
            sums.append(whole)
        for p, part in enumerate(unpacked(*sums)):
            k, at = p // 2, pl.ds(p % 2 * PART, PART)
            obj_out[s, k, at] = obj[s, k, at] - OBJECT_RATE * part[:, :TILE]

    update(1)

    my_share = pl.multiple_of(me * share, 8)

    def deep_copy(k, sender):
        return pltpu.make_async_remote_copy(
            src_ref=deep_in.at[z],
            dst_ref=deep_in.at[sender],
            send_sem=deep_s.at[k],
            recv_sem=deep_r.at[sender],
            device_id=in_depth(k),
            device_id_type=MESH,
        )

    @pl.when(me < owners)
    def _():
        whole = half_in[pl.ds(my_share, share)]
        for p in range(group):
            @pl.when(me != p)
            def _():
                plane_copy(0, p).wait_recv()
        plane_in[me] = whole
        whole = plane_in[0]
        for p in range(1, group):
            whole = whole + plane_in[p]
        deep_in[z] = whole
        for k in range(depth):
            @pl.when(z != k)
            def _():
                deep_copy(k, z).start()

    for i, j in AROUND:
        grad_copy(0, i, j).wait_recv()
    update(0)

    def back_copy(p, sender):
        at = pl.ds(pl.multiple_of(mine + sender * share, 8), share)
        return pltpu.make_async_remote_copy(
            src_ref=total.at[at],
            dst_ref=total.at[at],
            send_sem=back_s.at[p],
            recv_sem=back_r.at[sender],
            device_id=in_plane(p),
            device_id_type=MESH,
        )

    def last_copy(base, q):
        at = pl.ds(pl.multiple_of(base + q * share, 8), share)
        return pltpu.make_async_remote_copy(
            src_ref=total.at[at],
            dst_ref=total.at[at],
            send_sem=last_s.at[q],
            recv_sem=last_r.at[q],
            device_id=other,
            device_id_type=MESH,
        )

    @pl.when(me < owners)
    def _():
        for k in range(depth):
            @pl.when(z != k)
            def _():
                deep_copy(0, k).wait_recv()
        whole = deep_in[0]
        for k in range(1, depth):
            whole = whole + deep_in[k]
        total[pl.ds(pl.multiple_of(mine + my_share, 8), share)] = whole
        for p in range(group):
            @pl.when(me != p)
            def _():
                back_copy(p, me).start()

    for q in range(owners):
        @pl.when(me != q)
        def _():
            back_copy(0, q).wait_recv()
        last_copy(mine, q).start()
    for q in range(owners):
        last_copy(theirs, q).wait_recv()

    rate = PROBE_RATE / (SLOTS * rows * cols)

    def finish(at):
        d = pl.ds(at, step)
        re = total[d]
        im = total[pl.ds(WIDTH + at, step)]
        rest = total[pl.ds(2 * WIDTH + at, step)]
        probe_out[0, d, :128] = probe[0, d, :128] - rate * re
        probe_out[1, d, :128] = probe[1, d, :128] - rate * im
        probe_out[0, d, 128:] = probe[0, d, 128:] - rate * rest[:, :64]
        probe_out[1, d, 128:] = probe[1, d, 128:] - rate * pltpu.roll(rest, 64, 1)[:, :64]

    chunks(finish, step)

    for s in range(2):
        for i, j in AROUND:
            halo_copy(s, i, j).wait_send()
            grad_copy(s, i, j).wait_send()
    pair.wait_send()
    for q in range(owners):
        @pl.when(me != q)
        def _():
            plane_copy(q, me).wait_send()
        last_copy(mine, q).wait_send()

    @pl.when(me < owners)
    def _():
        for k in range(depth):
            @pl.when(z != k)
            def _():
                deep_copy(k, z).wait_send()
        for p in range(group):
            @pl.when(me != p)
            def _():
                back_copy(p, me).wait_send()


def solution(mesh):
    rows, cols = mesh.shape["row"], mesh.shape["col"]
    group, depth = 2 * cols, rows // 4
    share = -(-(HALF // 8) // group) * 8
    owners = HALF // share
    consts = matrices()

    def shards(object_slices, probe, propagator_phase, measured, offsets, counts):
        vmem = pl.BlockSpec(memory_space=pltpu.VMEM)
        dma = pltpu.SemaphoreType.DMA
        square = (WIDTH, LANES)
        return pl.pallas_call(
            functools.partial(kernel, rows, cols, share, owners),
            out_shape=(
                jax.ShapeDtypeStruct(object_slices.shape, F32),
                jax.ShapeDtypeStruct(probe.shape, F32),
            ),
            in_specs=[pl.BlockSpec(memory_space=pltpu.HBM)] * 10,
            out_specs=(vmem, vmem),
            scratch_shapes=[
                pltpu.SMEM((1, 1, SLOTS, 2), jnp.int32),
                pltpu.SMEM((1, 1), jnp.int32),
                pltpu.VMEM(object_slices.shape, F32),
                pltpu.VMEM(probe.shape, F32),
                pltpu.VMEM(propagator_phase.shape, F32),
                pltpu.VMEM(measured.shape[2:], F32),
                *[pltpu.VMEM(m.shape, BF16) for m in consts],
                dma((10,)),
                pltpu.VMEM((2, 2, TILE, 128), F32),
                pltpu.VMEM((2, 3, PART, 128), F32),
                pltpu.VMEM((2, 9, 3, PART, 128), F32),
                pltpu.VMEM((2, 3, 3 * TILE, 128), F32),
                pltpu.VMEM((2, SLOTS, 2) + square, F32),
                pltpu.VMEM((2,) + square, F32),
                pltpu.VMEM((2,) + square, F32),
                pltpu.VMEM((SLOTS * WIDTH, 2 * LANES), BF16),
                pltpu.VMEM((SLOTS * WIDTH, 2 * LANES), BF16),
                pltpu.VMEM((SLOTS, 2 * WIDTH, LANES), BF16),
                pltpu.VMEM((SLOTS, 2 * WIDTH, LANES), BF16),
                pltpu.VMEM((SLOTS, 2 * WIDTH, LANES), F32),
                pltpu.VMEM((SLOTS, 2) + square, F32),
                pltpu.VMEM((SLOTS, 2, 2, 4 * TILE, 128), F32),
                pltpu.VMEM((2, 9, 3, PART, 128), F32),
                pltpu.VMEM((2, 9, 3, PART, 128), F32),
                pltpu.VMEM((2 * HALF, 128), F32),
                pltpu.VMEM((HALF, 128), F32),
                pltpu.VMEM((group, share, 128), F32),
                pltpu.VMEM((depth, share, 128), F32),
                pltpu.VMEM((2 * HALF, 128), F32),
                dma((2, 9)), dma((2, 9)), dma((2, 9)), dma((2, 9)),
                dma, dma,
                dma((owners,)), dma((group,)),
                dma((depth,)), dma((depth,)),
                dma((group,)), dma((owners,)),
                dma((owners,)), dma((owners,)),
            ],
            compiler_params=pltpu.CompilerParams(
                collective_id=0, has_side_effects=True, vmem_limit_bytes=62 * 1024 * 1024
            ),
        )(
            offsets, counts, object_slices, probe, propagator_phase, measured,
            *[jnp.asarray(m) for m in consts],
        )

    return jax.shard_map(
        shards,
        mesh=mesh,
        in_specs=(
            P(None, None, "row", "col"),
            P(),
            P(),
            P("row", "col", None, None, None),
            P("row", "col", None, None),
            P("row", "col"),
        ),
        out_specs=(P(None, None, "row", "col"), P()),
        check_vma=False,
    )
```

```python
import functools

import jax
import jax.numpy as jnp
import ml_dtypes
import numpy as np
from jax import lax
from jax.experimental import pallas as pl
from jax.experimental.pallas import tpu as pltpu
from jax.sharding import PartitionSpec as P

OBJECT_RATE = 0.02
PROBE_RATE = 0.3
TILE = 96
WIDTH = 192
LANES = 256
SLOTS = 2
HALF = 288
PART = 48
MESH = pl.DeviceIdType.MESH
SIDES = (-1, 1)
AROUND = [(i, j) for i in (-1, 0, 1) for j in (-1, 0, 1) if (i, j) != (0, 0)]
F32 = jnp.float32
BF16 = jnp.bfloat16


def place(i, j):
    return (i + 1) * 3 + (j + 1)


def matrices():
    n = np.arange(WIDTH)
    angle = 2.0 * np.pi * (np.outer(n, n) % WIDTH) / WIDTH
    c = np.cos(angle) / np.sqrt(WIDTH)
    s = np.sin(angle) / np.sqrt(WIDTH)
    right = np.zeros((2 * LANES, 2 * LANES))
    right[:WIDTH, :WIDTH] = c
    right[:WIDTH, LANES : LANES + WIDTH] = -s
    right[LANES : LANES + WIDTH, :WIDTH] = s
    right[LANES : LANES + WIDTH, LANES : LANES + WIDTH] = c
    left = np.block([[c, s], [-s, c]])
    parts = []
    for full in (right, left):
        high = full.astype(np.float32).astype(ml_dtypes.bfloat16)
        low = (full - high.astype(np.float64)).astype(np.float32).astype(ml_dtypes.bfloat16)
        parts += [high, low]
    return parts


def two(x):
    high = x.astype(BF16)
    return high, (x - high.astype(F32)).astype(BF16)


def times(ar, ai, br, bi):
    return ar * br - ai * bi, ar * bi + ai * br


def times_conj(ar, ai, br, bi):
    return ar * br + ai * bi, ar * bi - ai * br


def packed(a, b, c, d):
    lane = lax.broadcasted_iota(jnp.int32, a.shape, 1)
    b, c, d = pltpu.roll(b, 96, 1), pltpu.roll(c, 64, 1), pltpu.roll(d, 32, 1)
    return jnp.where(lane < 96, a, b), jnp.where(lane < 64, b, c), jnp.where(lane < 32, c, d)


def unpacked(u, v, w):
    lane = lax.broadcasted_iota(jnp.int32, u.shape, 1)
    b = jnp.where(lane < 32, pltpu.roll(u, 32, 1), pltpu.roll(v, 32, 1))
    c = jnp.where(lane < 64, pltpu.roll(v, 64, 1), pltpu.roll(w, 64, 1))
    return u, b, c, pltpu.roll(w, 96, 1)


def dot(a, b):
    return jnp.dot(a, b, preferred_element_type=F32)


def chunks(body, step, total=WIDTH):
    for at in range(0, total, step):
        body(at)


def kernel(
    rows, cols, share, owners,
    offsets_in, counts_in, obj_in, probe_in, phase_in, measured_in, *rest,
):
    wide_in, (obj_out, probe_out), rest = rest[:4], rest[4:6], rest[6:]
    fetch(rows, cols, share, owners, offsets_in, counts_in, obj_in, probe_in, phase_in,
          measured_in, wide_in, obj_out, probe_out, *rest)


def fetch(
    rows, cols, share, owners,
    offsets_in, counts_in, obj_in, probe_in, phase_in, measured_in, wide_in,
    obj_out, probe_out,
    offsets, counts, obj, probe, phase, measured, wrh, wrl, wlh, wll, load,
    wide, halo, band, win, wave, trans, xh, xl, lh, ll, y, carried, shift,
    gsend, grow, gcol, pack, half_in, plane_in, deep_in, total,
    halo_s, halo_r, col_s, col_r, row_s, row_r, grow_s, grow_r, gcol_s, gcol_r, pair_s, pair_r, plane_s, plane_r, deep_s, deep_r,
    back_s, back_r, last_s, last_r,
):
    r = lax.axis_index("row")
    c = lax.axis_index("col")
    core = lax.rem(r, 2)
    x_lo = lax.rem(lax.div(r, 2), 2)
    z = lax.div(r, 4)
    depth = rows // 4
    group = 2 * cols
    me = x_lo * cols + c
    other = (r + 1 - 2 * core, c)

    def beside(i, j):
        return (lax.rem(r + i + rows, rows), lax.rem(c + j + cols, cols))

    def in_plane(p):
        return (z * 4 + (p // cols) * 2 + core, p % cols)

    def in_depth(k):
        return (k * 4 + x_lo * 2 + core, c)

    def inside(i, j):
        return (r + i >= 0) & (r + i < rows) & (c + j >= 0) & (c + j < cols)

    loads = [
        pltpu.make_async_copy(a, b, load.at[i])
        for i, (a, b) in enumerate(
            zip(
                (obj_in, offsets_in, counts_in, probe_in, phase_in, *wide_in, measured_in.at[0, 0]),
                (obj, offsets, counts, probe, phase, wrh, wrl, wlh, wll, measured),
            )
        )
    ]
    for one in loads:
        one.start()

    barrier = pltpu.get_barrier_semaphore()

    def greet(device):
        pl.semaphore_signal(barrier, inc=1, device_id=device, device_id_type=MESH)

    for i, j in AROUND:
        greet(beside(i, j))
    greet(other)
    for d in range(1, group):
        p = lax.rem(me + d, group)
        greet((z * 4 + lax.div(p, cols) * 2 + core, lax.rem(p, cols)))
    for d in range(1, depth):
        greet((lax.rem(z + d, depth) * 4 + x_lo * 2 + core, c))

    loads[0].wait()
    for s in range(2):
        quarters = []
        for k in range(2):
            wide[s, k] = jnp.zeros((TILE, 128), F32)
            wide[s, k, :, :TILE] = obj[s, k]
            quarters += [wide[s, k, :PART], wide[s, k, PART:]]
        for m, v in enumerate(packed(*quarters)):
            halo[s, place(0, 0), m] = v

    pl.semaphore_wait(barrier, len(AROUND) + group + depth - 1)

    def halo_copy(i, j):
        return pltpu.make_async_remote_copy(
            src_ref=halo.at[0, place(0, 0)],
            dst_ref=halo.at[0, place(-i, -j)],
            send_sem=halo_s.at[place(i, j)],
            recv_sem=halo_r.at[place(-i, -j)],
            device_id=beside(i, j),
            device_id_type=MESH,
        )

    def col_copy(j):
        return pltpu.make_async_remote_copy(
            src_ref=halo.at[1, place(0, 0)],
            dst_ref=halo.at[1, place(0, -j)],
            send_sem=col_s.at[j + 1],
            recv_sem=col_r.at[1 - j],
            device_id=beside(0, j),
            device_id_type=MESH,
        )

    def row_copy(i):
        return pltpu.make_async_remote_copy(
            src_ref=halo.at[1, pl.ds(place(0, -1), 3)],
            dst_ref=halo.at[1, pl.ds(place(-i, -1), 3)],
            send_sem=row_s.at[i + 1],
            recv_sem=row_r.at[1 - i],
            device_id=beside(i, 0),
            device_id_type=MESH,
        )

    def grad_row(s, i):
        return pltpu.make_async_remote_copy(
            src_ref=gsend.at[s, pl.ds(place(i, -1), 3)],
            dst_ref=grow.at[s, 1 - i],
            send_sem=grow_s.at[s, i + 1],
            recv_sem=grow_r.at[s, 1 - i],
            device_id=beside(i, 0),
            device_id_type=MESH,
        )

    def grad_col(s, j):
        return pltpu.make_async_remote_copy(
            src_ref=gsend.at[s, place(0, j)],
            dst_ref=gcol.at[s, 1 - j],
            send_sem=gcol_s.at[s, j + 1],
            recv_sem=gcol_r.at[s, 1 - j],
            device_id=beside(0, j),
            device_id_type=MESH,
        )

    for i, j in AROUND:
        halo_copy(i, j).start()
    for j in SIDES:
        col_copy(j).start()

    for one in loads[1:]:
        one.wait()
    for k in range(2):
        wave[k] = jnp.zeros((WIDTH, LANES), F32)
        wave[k, :, :WIDTH] = probe[k]
        trans[k] = jnp.zeros((WIDTH, LANES), F32)
    trans[0, :, :WIDTH] = jnp.cos(phase[...])
    trans[1, :, :WIDTH] = jnp.sin(phase[...])
    for slot in range(SLOTS):
        for k in range(2):
            for m in range(2):
                shift[slot, k, m, :TILE] = jnp.zeros((TILE, 128), F32)
                shift[slot, k, m, TILE + WIDTH :] = jnp.zeros((TILE, 128), F32)

    ro = [offsets[0, 0, slot, 0] for slot in range(SLOTS)]
    co = [offsets[0, 0, slot, 1] for slot in range(SLOTS)]
    live = [slot < counts[0, 0] for slot in range(SLOTS)]

    def windows(s):
        lane = lax.broadcasted_iota(jnp.int32, (PART, 128), 1)
        for i in (-1, 0, 1):
            tiles = []
            for j in (-1, 0, 1):
                if (i, j) == (0, 0):
                    tiles.append(unpacked(*[halo[s, place(0, 0), m] for m in range(3)]))
                else:
                    keep = inside(i, j)
                    tiles.append(
                        unpacked(
                            *[jnp.where(keep, halo[s, place(i, j), m], 0.0) for m in range(3)]
                        )
                    )
            for k in range(2):
                for h in range(2):
                    a, b, d = [tile[2 * k + h] for tile in tiles]
                    b = pltpu.roll(b, 96, 1)
                    d = pltpu.roll(d, 64, 1)
                    at = pl.ds((i + 1) * TILE + h * PART, PART)
                    band[k, 0, at] = jnp.where(lane < 96, a, b)
                    band[k, 1, at] = jnp.where(lane < 64, b, d)
                    band[k, 2, at] = jnp.where(lane < 64, d, 0.0)
        for slot in range(SLOTS):
            for k in range(2):
                lane = lax.broadcasted_iota(jnp.int32, (WIDTH, 128), 1)
                turn = lax.rem(128 - co[slot], 128)
                at = pl.ds(ro[slot], WIDTH)
                v = [pltpu.roll(band[k, m, at], turn, 1) for m in range(3)]
                keep = lane < 128 - co[slot]
                win[s, slot, k, :, 0:128] = jnp.where(keep, v[0], v[1])
                win[s, slot, k, :, 128:256] = jnp.where(keep, v[1], v[2])

    def put(slot, at, step, re, im, inverse):
        if inverse:
            re, im = im, re
        to = pl.ds(slot * WIDTH + at, step)
        xh[to, :LANES], xl[to, :LANES] = two(re)
        xh[to, LANES:], xl[to, LANES:] = two(im)

    def transform():
        acc = dot(xh[...], wrh[...]) + dot(xl[...], wrh[...]) + dot(xh[...], wrl[...])
        for slot in range(SLOTS):
            part = acc[slot * WIDTH : (slot + 1) * WIDTH]
            lh[slot, :WIDTH], ll[slot, :WIDTH] = two(part[:, :LANES])
            lh[slot, WIDTH:], ll[slot, WIDTH:] = two(part[:, LANES:])
        for slot in range(SLOTS):
            y[slot] = (
                dot(wlh[...], lh[slot]) + dot(wlh[...], ll[slot]) + dot(wll[...], lh[slot])
            )

    def got(slot, at, step, inverse):
        one = y[slot, pl.ds(at, step), :]
        two_ = y[slot, pl.ds(WIDTH + at, step), :]
        return (two_, one) if inverse else (one, two_)

    step = 32

    def each(body):
        for slot in range(SLOTS):
            chunks(functools.partial(body, slot), step)

    def spread(s):
        lane = lax.broadcasted_iota(jnp.int32, (PART, 128), 1)
        for i in (-1, 0, 1):
            tiles = ([], [], [])
            for k in range(2):
                for h in range(2):
                    v = [0.0, 0.0, 0.0]
                    for slot in range(SLOTS):
                        at = pl.ds(TILE * (i + 2) + PART * h - ro[slot], PART)
                        a = pltpu.roll(shift[slot, k, 0, at], co[slot], 1)
                        b = pltpu.roll(shift[slot, k, 1, at], co[slot], 1)
                        wrap = lane < co[slot]
                        v[0] = v[0] + jnp.where(wrap, 0.0, a)
                        v[1] = v[1] + jnp.where(wrap, a, b)
                        v[2] = v[2] + jnp.where(wrap, b, 0.0)
                    tiles[0].append(v[0])
                    tiles[1].append(
                        jnp.where(lane < 32, pltpu.roll(v[0], 32, 1), pltpu.roll(v[1], 32, 1))
                    )
                    tiles[2].append(
                        jnp.where(lane < 64, pltpu.roll(v[1], 64, 1), pltpu.roll(v[2], 64, 1))
                    )
            for j in (-1, 0, 1):
                for m, part in enumerate(packed(*tiles[j + 1])):
                    gsend[s, place(i, j), m] = part

    def shifted(slot, at, re, im):
        to = pl.ds(TILE + at, step)
        for k, part in enumerate((re, im)):
            part = jnp.where(live[slot], part, 0.0)
            shift[slot, k, 0, to] = part[:, :128]
            shift[slot, k, 1, to] = part[:, 128:]

    for i, j in AROUND:
        halo_copy(i, j).wait_recv()
    for j in SIDES:
        col_copy(j).wait_recv()
    for i in SIDES:
        row_copy(i).start()
    windows(0)

    def enter(slot, at):
        d = pl.ds(at, step)
        re, im = times(wave[0, d], wave[1, d], win[0, slot, 0, d], win[0, slot, 1, d])
        put(slot, at, step, re, im, False)

    each(enter)
    transform()

    def carry(slot, at):
        d = pl.ds(at, step)
        re, im = got(slot, at, step, False)
        re, im = times(trans[0, d], trans[1, d], re, im)
        put(slot, at, step, re, im, True)

    each(carry)
    transform()

    for i in SIDES:
        row_copy(i).wait_recv()
    windows(1)

    def leave(slot, at):
        d = pl.ds(at, step)
        re, im = got(slot, at, step, True)
        carried[slot, 0, d] = re
        carried[slot, 1, d] = im
        re, im = times(re, im, win[1, slot, 0, d], win[1, slot, 1, d])
        put(slot, at, step, re, im, False)

    each(leave)
    transform()

    def residual(slot, at):
        re, im = got(slot, at, step, False)
        seen = jnp.concatenate(
            [measured[slot, pl.ds(at, step), :], jnp.zeros((step, LANES - WIDTH), F32)], axis=1
        )
        resid = re * re + im * im - seen
        put(slot, at, step, resid * re, resid * im, True)

    each(residual)
    transform()

    def second(slot, at):
        d = pl.ds(at, step)
        re, im = got(slot, at, step, True)
        shifted(slot, at, *times_conj(carried[slot, 0, d], carried[slot, 1, d], re, im))
        re, im = times_conj(win[1, slot, 0, d], win[1, slot, 1, d], re, im)
        put(slot, at, step, re, im, False)

    each(second)
    spread(1)
    for i in SIDES:
        grad_row(1, i).start()
    transform()

    def inner(slot, at):
        d = pl.ds(at, step)
        re, im = got(slot, at, step, False)
        re, im = times_conj(trans[0, d], trans[1, d], re, im)
        put(slot, at, step, re, im, True)

    each(inner)
    transform()

    def probe_part(at):
        d = pl.ds(at, step)
        re = jnp.zeros((step, LANES), F32)
        im = jnp.zeros((step, LANES), F32)
        for slot in range(SLOTS):
            ir, ii = got(slot, at, step, True)
            pr, pi = times_conj(win[0, slot, 0, d], win[0, slot, 1, d], ir, ii)
            re = re + jnp.where(live[slot], pr, 0.0)
            im = im + jnp.where(live[slot], pi, 0.0)
            shifted(slot, at, *times_conj(wave[0, d], wave[1, d], ir, ii))
        lane = lax.broadcasted_iota(jnp.int32, (step, 128), 1)
        pack[d] = re[:, :128]
        pack[pl.ds(WIDTH + at, step)] = im[:, :128]
        pack[pl.ds(2 * WIDTH + at, step)] = jnp.where(
            lane < 64, re[:, 128:], pltpu.roll(im[:, 128:], 64, 1)
        )

    chunks(probe_part, step)

    mine = pl.multiple_of(HALF * core, 8)
    theirs = pl.multiple_of(HALF * (1 - core), 8)
    pair = pltpu.make_async_remote_copy(
        src_ref=pack.at[pl.ds(theirs, HALF)],
        dst_ref=half_in,
        send_sem=pair_s,
        recv_sem=pair_r,
        device_id=other,
        device_id_type=MESH,
    )
    pair.start()

    spread(0)

    def fold(s):
        for i in SIDES:
            grad_row(s, i).wait_recv()
        for j in (-1, 1, 0):
            for m in range(3):
                whole = gsend[s, place(0, j), m]
                for i in SIDES:
                    keep = (r + i >= 0) & (r + i < rows)
                    whole = whole + jnp.where(keep, grow[s, i + 1, j + 1, m], 0.0)
                gsend[s, place(0, j), m] = whole
            if j != 0:
                grad_col(s, j).start()

    pair.wait_recv()
    half_in[...] = half_in[...] + pack[pl.ds(mine, HALF)]

    def plane_copy(q, sender):
        return pltpu.make_async_remote_copy(
            src_ref=half_in.at[pl.ds(q * share, share)],
            dst_ref=plane_in.at[sender],
            send_sem=plane_s.at[q],
            recv_sem=plane_r.at[sender],
            device_id=in_plane(q),
            device_id_type=MESH,
        )

    for q in range(owners):
        @pl.when(me != q)
        def _():
            plane_copy(q, me).start()

    fold(1)
    for i in SIDES:
        grad_row(0, i).start()

    def update(s):
        for j in SIDES:
            grad_col(s, j).wait_recv()
        sums = []
        for m in range(3):
            whole = gsend[s, place(0, 0), m]
            for j in SIDES:
                keep = (c + j >= 0) & (c + j < cols)
                whole = whole + jnp.where(keep, gcol[s, j + 1, m], 0.0)
            sums.append(whole)
        for p, part in enumerate(unpacked(*sums)):
            k, at = p // 2, pl.ds(p % 2 * PART, PART)
            obj_out[s, k, at] = obj[s, k, at] - OBJECT_RATE * part[:, :TILE]

    my_share = pl.multiple_of(me * share, 8)

    def deep_copy(k, sender):
        return pltpu.make_async_remote_copy(
            src_ref=deep_in.at[z],
            dst_ref=deep_in.at[sender],
            send_sem=deep_s.at[k],
            recv_sem=deep_r.at[sender],
            device_id=in_depth(k),
            device_id_type=MESH,
        )

    @pl.when(me < owners)
    def _():
        whole = half_in[pl.ds(my_share, share)]
        for p in range(group):
            @pl.when(me != p)
            def _():
                plane_copy(0, p).wait_recv()
        plane_in[me] = whole
        whole = plane_in[0]
        for p in range(1, group):
            whole = whole + plane_in[p]
        deep_in[z] = whole
        for k in range(depth):
            @pl.when(z != k)
            def _():
                deep_copy(k, z).start()

    fold(0)
    update(1)

    def back_copy(p, sender):
        at = pl.ds(pl.multiple_of(mine + sender * share, 8), share)
        return pltpu.make_async_remote_copy(
            src_ref=total.at[at],
            dst_ref=total.at[at],
            send_sem=back_s.at[p],
            recv_sem=back_r.at[sender],
            device_id=in_plane(p),
            device_id_type=MESH,
        )

    def last_copy(base, q):
        at = pl.ds(pl.multiple_of(base + q * share, 8), share)
        return pltpu.make_async_remote_copy(
            src_ref=total.at[at],
            dst_ref=total.at[at],
            send_sem=last_s.at[q],
            recv_sem=last_r.at[q],
            device_id=other,
            device_id_type=MESH,
        )

    @pl.when(me < owners)
    def _():
        for k in range(depth):
            @pl.when(z != k)
            def _():
                deep_copy(0, k).wait_recv()
        whole = deep_in[0]
        for k in range(1, depth):
            whole = whole + deep_in[k]
        total[pl.ds(pl.multiple_of(mine + my_share, 8), share)] = whole
        for p in range(group):
            @pl.when(me != p)
            def _():
                back_copy(p, me).start()

    update(0)

    for q in range(owners):
        @pl.when(me != q)
        def _():
            back_copy(0, q).wait_recv()
        last_copy(mine, q).start()
    for q in range(owners):
        last_copy(theirs, q).wait_recv()

    rate = PROBE_RATE / (SLOTS * rows * cols)

    def finish(at):
        d = pl.ds(at, step)
        re = total[d]
        im = total[pl.ds(WIDTH + at, step)]
        rest = total[pl.ds(2 * WIDTH + at, step)]
        probe_out[0, d, :128] = probe[0, d, :128] - rate * re
        probe_out[1, d, :128] = probe[1, d, :128] - rate * im
        probe_out[0, d, 128:] = probe[0, d, 128:] - rate * rest[:, :64]
        probe_out[1, d, 128:] = probe[1, d, 128:] - rate * pltpu.roll(rest, 64, 1)[:, :64]

    chunks(finish, step)

    for i, j in AROUND:
        halo_copy(i, j).wait_send()
    for i in SIDES:
        col_copy(i).wait_send()
        row_copy(i).wait_send()
        for s in range(2):
            grad_row(s, i).wait_send()
            grad_col(s, i).wait_send()
    pair.wait_send()
    for q in range(owners):
        @pl.when(me != q)
        def _():
            plane_copy(q, me).wait_send()
        last_copy(mine, q).wait_send()

    @pl.when(me < owners)
    def _():
        for k in range(depth):
            @pl.when(z != k)
            def _():
                deep_copy(k, z).wait_send()
        for p in range(group):
            @pl.when(me != p)
            def _():
                back_copy(p, me).wait_send()


def solution(mesh):
    rows, cols = mesh.shape["row"], mesh.shape["col"]
    group, depth = 2 * cols, rows // 4
    share = -(-(HALF // 8) // group) * 8
    owners = HALF // share
    consts = matrices()

    def shards(object_slices, probe, propagator_phase, measured, offsets, counts):
        vmem = pl.BlockSpec(memory_space=pltpu.VMEM)
        dma = pltpu.SemaphoreType.DMA
        square = (WIDTH, LANES)
        return pl.pallas_call(
            functools.partial(kernel, rows, cols, share, owners),
            out_shape=(
                jax.ShapeDtypeStruct(object_slices.shape, F32),
                jax.ShapeDtypeStruct(probe.shape, F32),
            ),
            in_specs=[pl.BlockSpec(memory_space=pltpu.HBM)] * 10,
            out_specs=(vmem, vmem),
            scratch_shapes=[
                pltpu.SMEM((1, 1, SLOTS, 2), jnp.int32),
                pltpu.SMEM((1, 1), jnp.int32),
                pltpu.VMEM(object_slices.shape, F32),
                pltpu.VMEM(probe.shape, F32),
                pltpu.VMEM(propagator_phase.shape, F32),
                pltpu.VMEM(measured.shape[2:], F32),
                *[pltpu.VMEM(m.shape, BF16) for m in consts],
                dma((10,)),
                pltpu.VMEM((2, 2, TILE, 128), F32),
                pltpu.VMEM((2, 9, 3, PART, 128), F32),
                pltpu.VMEM((2, 3, 3 * TILE, 128), F32),
                pltpu.VMEM((2, SLOTS, 2) + square, F32),
                pltpu.VMEM((2,) + square, F32),
                pltpu.VMEM((2,) + square, F32),
                pltpu.VMEM((SLOTS * WIDTH, 2 * LANES), BF16),
                pltpu.VMEM((SLOTS * WIDTH, 2 * LANES), BF16),
                pltpu.VMEM((SLOTS, 2 * WIDTH, LANES), BF16),
                pltpu.VMEM((SLOTS, 2 * WIDTH, LANES), BF16),
                pltpu.VMEM((SLOTS, 2 * WIDTH, LANES), F32),
                pltpu.VMEM((SLOTS, 2) + square, F32),
                pltpu.VMEM((SLOTS, 2, 2, 4 * TILE, 128), F32),
                pltpu.VMEM((2, 9, 3, PART, 128), F32),
                pltpu.VMEM((2, 3, 3, 3, PART, 128), F32),
                pltpu.VMEM((2, 3, 3, PART, 128), F32),
                pltpu.VMEM((2 * HALF, 128), F32),
                pltpu.VMEM((HALF, 128), F32),
                pltpu.VMEM((group, share, 128), F32),
                pltpu.VMEM((depth, share, 128), F32),
                pltpu.VMEM((2 * HALF, 128), F32),
                dma((9,)), dma((9,)),
                dma((3,)), dma((3,)), dma((3,)), dma((3,)),
                dma((2, 3)), dma((2, 3)), dma((2, 3)), dma((2, 3)),
                dma, dma,
                dma((owners,)), dma((group,)),
                dma((depth,)), dma((depth,)),
                dma((group,)), dma((owners,)),
                dma((owners,)), dma((owners,)),
            ],
            compiler_params=pltpu.CompilerParams(
                collective_id=0, has_side_effects=True, vmem_limit_bytes=62 * 1024 * 1024
            ),
        )(
            offsets, counts, object_slices, probe, propagator_phase, measured,
            *[jnp.asarray(m) for m in consts],
        )

    return jax.shard_map(
        shards,
        mesh=mesh,
        in_specs=(
            P(None, None, "row", "col"),
            P(),
            P(),
            P("row", "col", None, None, None),
            P("row", "col", None, None),
            P("row", "col"),
        ),
        out_specs=(P(None, None, "row", "col"), P()),
        check_vma=False,
    )
```

```python
import functools

import jax
import jax.numpy as jnp
import ml_dtypes
import numpy as np
from jax import lax
from jax.experimental import pallas as pl
from jax.experimental.pallas import tpu as pltpu
from jax.sharding import PartitionSpec as P

OBJECT_RATE = 0.02
PROBE_RATE = 0.3
TILE = 96
WIDTH = 192
LANES = 256
SLOTS = 2
HALF = 288
PART = 48
MESH = pl.DeviceIdType.MESH
SIDES = (-1, 1)
AROUND = [(-1, -1), (-1, 1), (1, -1), (1, 1), (0, -1), (0, 1), (-1, 0), (1, 0)]
F32 = jnp.float32
BF16 = jnp.bfloat16


def place(i, j):
    return (i + 1) * 3 + (j + 1)


def matrices():
    n = np.arange(WIDTH)
    angle = 2.0 * np.pi * (np.outer(n, n) % WIDTH) / WIDTH
    c = np.cos(angle) / np.sqrt(WIDTH)
    s = np.sin(angle) / np.sqrt(WIDTH)
    right = np.zeros((2 * LANES, 2 * LANES))
    right[:WIDTH, :WIDTH] = c
    right[:WIDTH, LANES : LANES + WIDTH] = -s
    right[LANES : LANES + WIDTH, :WIDTH] = s
    right[LANES : LANES + WIDTH, LANES : LANES + WIDTH] = c
    left = np.block([[c, s], [-s, c]])
    parts = []
    for full in (right, left):
        high = full.astype(np.float32).astype(ml_dtypes.bfloat16)
        low = (full - high.astype(np.float64)).astype(np.float32).astype(ml_dtypes.bfloat16)
        parts += [high, low]
    return parts[:2] + [np.concatenate([parts[2], parts[2], parts[3]], axis=1)]


def two(x):
    high = x.astype(BF16)
    return high, (x - high.astype(F32)).astype(BF16)


def times(ar, ai, br, bi):
    return ar * br - ai * bi, ar * bi + ai * br


def times_conj(ar, ai, br, bi):
    return ar * br + ai * bi, ar * bi - ai * br


def packed(a, b, c, d):
    lane = lax.broadcasted_iota(jnp.int32, a.shape, 1)
    b, c, d = pltpu.roll(b, 96, 1), pltpu.roll(c, 64, 1), pltpu.roll(d, 32, 1)
    return jnp.where(lane < 96, a, b), jnp.where(lane < 64, b, c), jnp.where(lane < 32, c, d)


def unpacked(u, v, w):
    lane = lax.broadcasted_iota(jnp.int32, u.shape, 1)
    b = jnp.where(lane < 32, pltpu.roll(u, 32, 1), pltpu.roll(v, 32, 1))
    c = jnp.where(lane < 64, pltpu.roll(v, 64, 1), pltpu.roll(w, 64, 1))
    return u, b, c, pltpu.roll(w, 96, 1)


def dot(a, b):
    return jnp.dot(a, b, preferred_element_type=F32)


def chunks(body, step, total=WIDTH):
    for at in range(0, total, step):
        body(at)


def kernel(
    rows, cols, share, owners,
    offsets_in, counts_in, obj_in, probe_in, phase_in, measured_in, *rest,
):
    wide_in, (obj_out, probe_out), rest = rest[:3], rest[3:5], rest[5:]
    fetch(rows, cols, share, owners, offsets_in, counts_in, obj_in, probe_in, phase_in,
          measured_in, wide_in, obj_out, probe_out, *rest)


def fetch(
    rows, cols, share, owners,
    offsets_in, counts_in, obj_in, probe_in, phase_in, measured_in, wide_in,
    obj_out, probe_out,
    offsets, counts, obj, probe, phase, measured, wrh, wrl, wl, load,
    wide, halo, band, win, wave, trans, xh, xl, lh, y, carried, shift,
    gsend, grow, gcol, pack, half_in, plane_in, deep_in, total,
    halo_s, halo_r, col_s, col_r, row_s, row_r, grow_s, grow_r, gcol_s, gcol_r, pair_s, pair_r, plane_s, plane_r, deep_s, deep_r,
    back_s, back_r, last_s, last_r,
):
    r = lax.axis_index("row")
    c = lax.axis_index("col")
    core = lax.rem(r, 2)
    x_lo = lax.rem(lax.div(r, 2), 2)
    z = lax.div(r, 4)
    depth = rows // 4
    group = 2 * cols
    me = x_lo * cols + c
    other = (r + 1 - 2 * core, c)

    def beside(i, j):
        return (lax.rem(r + i + rows, rows), lax.rem(c + j + cols, cols))

    def in_plane(p):
        return (z * 4 + (p // cols) * 2 + core, p % cols)

    def in_depth(k):
        return (k * 4 + x_lo * 2 + core, c)

    def inside(i, j):
        return (r + i >= 0) & (r + i < rows) & (c + j >= 0) & (c + j < cols)

    loads = [
        pltpu.make_async_copy(a, b, load.at[i])
        for i, (a, b) in enumerate(
            zip(
                (obj_in, offsets_in, counts_in, probe_in, phase_in, *wide_in, measured_in.at[0, 0]),
                (obj, offsets, counts, probe, phase, wrh, wrl, wl, measured),
            )
        )
    ]
    for one in loads:
        one.start()

    barrier = pltpu.get_barrier_semaphore()

    def greet(device):
        pl.semaphore_signal(barrier, inc=1, device_id=device, device_id_type=MESH)

    for i, j in AROUND:
        greet(beside(i, j))
    greet(other)
    for d in range(1, group):
        p = lax.rem(me + d, group)
        greet((z * 4 + lax.div(p, cols) * 2 + core, lax.rem(p, cols)))
    for d in range(1, depth):
        greet((lax.rem(z + d, depth) * 4 + x_lo * 2 + core, c))

    loads[0].wait()
    for s in range(2):
        quarters = []
        for k in range(2):
            wide[s, k] = jnp.zeros((TILE, 128), F32)
            wide[s, k, :, :TILE] = obj[s, k]
            quarters += [wide[s, k, :PART], wide[s, k, PART:]]
        for m, v in enumerate(packed(*quarters)):
            halo[s, place(0, 0), m] = v

    pl.semaphore_wait(barrier, len(AROUND) + group + depth - 1)

    def halo_copy(i, j):
        return pltpu.make_async_remote_copy(
            src_ref=halo.at[0, place(0, 0)],
            dst_ref=halo.at[0, place(-i, -j)],
            send_sem=halo_s.at[place(i, j)],
            recv_sem=halo_r.at[place(-i, -j)],
            device_id=beside(i, j),
            device_id_type=MESH,
        )

    def col_copy(j):
        return pltpu.make_async_remote_copy(
            src_ref=halo.at[1, place(0, 0)],
            dst_ref=halo.at[1, place(0, -j)],
            send_sem=col_s.at[j + 1],
            recv_sem=col_r.at[1 - j],
            device_id=beside(0, j),
            device_id_type=MESH,
        )

    def row_copy(i):
        return pltpu.make_async_remote_copy(
            src_ref=halo.at[1, pl.ds(place(0, -1), 3)],
            dst_ref=halo.at[1, pl.ds(place(-i, -1), 3)],
            send_sem=row_s.at[i + 1],
            recv_sem=row_r.at[1 - i],
            device_id=beside(i, 0),
            device_id_type=MESH,
        )

    def grad_row(s, i):
        return pltpu.make_async_remote_copy(
            src_ref=gsend.at[s, pl.ds(place(i, -1), 3)],
            dst_ref=grow.at[s, 1 - i],
            send_sem=grow_s.at[s, i + 1],
            recv_sem=grow_r.at[s, 1 - i],
            device_id=beside(i, 0),
            device_id_type=MESH,
        )

    def grad_col(s, j):
        return pltpu.make_async_remote_copy(
            src_ref=gsend.at[s, place(0, j)],
            dst_ref=gcol.at[s, 1 - j],
            send_sem=gcol_s.at[s, j + 1],
            recv_sem=gcol_r.at[s, 1 - j],
            device_id=beside(0, j),
            device_id_type=MESH,
        )

    for j in SIDES:
        col_copy(j).start()
    for i, j in AROUND:
        halo_copy(i, j).start()

    for one in loads[1:]:
        one.wait()
    for k in range(2):
        wave[k] = jnp.zeros((WIDTH, LANES), F32)
        wave[k, :, :WIDTH] = probe[k]
        trans[k] = jnp.zeros((WIDTH, LANES), F32)
    trans[0, :, :WIDTH] = jnp.cos(phase[...])
    trans[1, :, :WIDTH] = jnp.sin(phase[...])
    for slot in range(SLOTS):
        for k in range(2):
            for m in range(2):
                shift[slot, k, m, :TILE] = jnp.zeros((TILE, 128), F32)
                shift[slot, k, m, TILE + WIDTH :] = jnp.zeros((TILE, 128), F32)

    ro = [offsets[0, 0, slot, 0] for slot in range(SLOTS)]
    co = [offsets[0, 0, slot, 1] for slot in range(SLOTS)]
    live = [slot < counts[0, 0] for slot in range(SLOTS)]

    def windows(s):
        lane = lax.broadcasted_iota(jnp.int32, (PART, 128), 1)
        for i in (-1, 0, 1):
            tiles = []
            for j in (-1, 0, 1):
                if (i, j) == (0, 0):
                    tiles.append(unpacked(*[halo[s, place(0, 0), m] for m in range(3)]))
                else:
                    keep = inside(i, j)
                    tiles.append(
                        unpacked(
                            *[jnp.where(keep, halo[s, place(i, j), m], 0.0) for m in range(3)]
                        )
                    )
            for k in range(2):
                for h in range(2):
                    a, b, d = [tile[2 * k + h] for tile in tiles]
                    b = pltpu.roll(b, 96, 1)
                    d = pltpu.roll(d, 64, 1)
                    at = pl.ds((i + 1) * TILE + h * PART, PART)
                    band[k, 0, at] = jnp.where(lane < 96, a, b)
                    band[k, 1, at] = jnp.where(lane < 64, b, d)
                    band[k, 2, at] = jnp.where(lane < 64, d, 0.0)
        for slot in range(SLOTS):
            for k in range(2):
                lane = lax.broadcasted_iota(jnp.int32, (WIDTH, 128), 1)
                turn = lax.rem(128 - co[slot], 128)
                at = pl.ds(ro[slot], WIDTH)
                v = [pltpu.roll(band[k, m, at], turn, 1) for m in range(3)]
                keep = lane < 128 - co[slot]
                win[s, slot, k, :, 0:128] = jnp.where(keep, v[0], v[1])
                win[s, slot, k, :, 128:256] = jnp.where(keep, v[1], v[2])

    def put(slot, at, step, re, im, inverse):
        if inverse:
            re, im = im, re
        to = pl.ds(slot * WIDTH + at, step)
        xh[to, :LANES], xl[to, :LANES] = two(re)
        xh[to, LANES:], xl[to, LANES:] = two(im)

    def transform():
        acc = dot(xh[...], wrh[...]) + dot(xl[...], wrh[...]) + dot(xh[...], wrl[...])
        for slot in range(SLOTS):
            part = acc[slot * WIDTH : (slot + 1) * WIDTH]
            for k in range(2):
                high, low = two(part[:, k * LANES : (k + 1) * LANES])
                for m, piece in enumerate((high, low, high)):
                    at = 2 * m * WIDTH + k * WIDTH
                    lh[slot, at : at + WIDTH] = piece
        for slot in range(SLOTS):
            y[slot] = dot(wl[...], lh[slot])

    def got(slot, at, step, inverse):
        one = y[slot, pl.ds(at, step), :]
        two_ = y[slot, pl.ds(WIDTH + at, step), :]
        return (two_, one) if inverse else (one, two_)

    step = 32

    def each(body):
        for slot in range(SLOTS):
            chunks(functools.partial(body, slot), step)

    def spread(s):
        lane = lax.broadcasted_iota(jnp.int32, (PART, 128), 1)
        for i in (-1, 0, 1):
            tiles = ([], [], [])
            for k in range(2):
                for h in range(2):
                    v = [0.0, 0.0, 0.0]
                    for slot in range(SLOTS):
                        at = pl.ds(TILE * (i + 2) + PART * h - ro[slot], PART)
                        a = pltpu.roll(shift[slot, k, 0, at], co[slot], 1)
                        b = pltpu.roll(shift[slot, k, 1, at], co[slot], 1)
                        wrap = lane < co[slot]
                        v[0] = v[0] + jnp.where(wrap, 0.0, a)
                        v[1] = v[1] + jnp.where(wrap, a, b)
                        v[2] = v[2] + jnp.where(wrap, b, 0.0)
                    tiles[0].append(v[0])
                    tiles[1].append(
                        jnp.where(lane < 32, pltpu.roll(v[0], 32, 1), pltpu.roll(v[1], 32, 1))
                    )
                    tiles[2].append(
                        jnp.where(lane < 64, pltpu.roll(v[1], 64, 1), pltpu.roll(v[2], 64, 1))
                    )
            for j in (-1, 0, 1):
                for m, part in enumerate(packed(*tiles[j + 1])):
                    gsend[s, place(i, j), m] = part

    def shifted(slot, at, re, im):
        to = pl.ds(TILE + at, step)
        for k, part in enumerate((re, im)):
            part = jnp.where(live[slot], part, 0.0)
            shift[slot, k, 0, to] = part[:, :128]
            shift[slot, k, 1, to] = part[:, 128:]

    for j in SIDES:
        col_copy(j).wait_recv()
    for i in SIDES:
        row_copy(i).start()
    for i, j in AROUND:
        halo_copy(i, j).wait_recv()
    windows(0)

    def enter(slot, at):
        d = pl.ds(at, step)
        re, im = times(wave[0, d], wave[1, d], win[0, slot, 0, d], win[0, slot, 1, d])
        put(slot, at, step, re, im, False)

    each(enter)
    transform()

    def carry(slot, at):
        d = pl.ds(at, step)
        re, im = got(slot, at, step, False)
        re, im = times(trans[0, d], trans[1, d], re, im)
        put(slot, at, step, re, im, True)

    each(carry)
    transform()

    for i in SIDES:
        row_copy(i).wait_recv()
    windows(1)

    def leave(slot, at):
        d = pl.ds(at, step)
        re, im = got(slot, at, step, True)
        carried[slot, 0, d] = re
        carried[slot, 1, d] = im
        re, im = times(re, im, win[1, slot, 0, d], win[1, slot, 1, d])
        put(slot, at, step, re, im, False)

    each(leave)
    transform()

    def residual(slot, at):
        re, im = got(slot, at, step, False)
        seen = jnp.concatenate(
            [measured[slot, pl.ds(at, step), :], jnp.zeros((step, LANES - WIDTH), F32)], axis=1
        )
        resid = re * re + im * im - seen
        put(slot, at, step, resid * re, resid * im, True)

    each(residual)
    transform()

    def second(slot, at):
        d = pl.ds(at, step)
        re, im = got(slot, at, step, True)
        shifted(slot, at, *times_conj(carried[slot, 0, d], carried[slot, 1, d], re, im))
        re, im = times_conj(win[1, slot, 0, d], win[1, slot, 1, d], re, im)
        put(slot, at, step, re, im, False)

    each(second)
    spread(1)
    for i in SIDES:
        grad_row(1, i).start()
    transform()

    def inner(slot, at):
        d = pl.ds(at, step)
        re, im = got(slot, at, step, False)
        re, im = times_conj(trans[0, d], trans[1, d], re, im)
        put(slot, at, step, re, im, True)

    each(inner)
    transform()

    def probe_part(at):
        d = pl.ds(at, step)
        re = jnp.zeros((step, LANES), F32)
        im = jnp.zeros((step, LANES), F32)
        for slot in range(SLOTS):
            ir, ii = got(slot, at, step, True)
            pr, pi = times_conj(win[0, slot, 0, d], win[0, slot, 1, d], ir, ii)
            re = re + jnp.where(live[slot], pr, 0.0)
            im = im + jnp.where(live[slot], pi, 0.0)
            shifted(slot, at, *times_conj(wave[0, d], wave[1, d], ir, ii))
        lane = lax.broadcasted_iota(jnp.int32, (step, 128), 1)
        pack[d] = re[:, :128]
        pack[pl.ds(WIDTH + at, step)] = im[:, :128]
        pack[pl.ds(2 * WIDTH + at, step)] = jnp.where(
            lane < 64, re[:, 128:], pltpu.roll(im[:, 128:], 64, 1)
        )

    chunks(probe_part, step)

    mine = pl.multiple_of(HALF * core, 8)
    theirs = pl.multiple_of(HALF * (1 - core), 8)
    pair = pltpu.make_async_remote_copy(
        src_ref=pack.at[pl.ds(theirs, HALF)],
        dst_ref=half_in,
        send_sem=pair_s,
        recv_sem=pair_r,
        device_id=other,
        device_id_type=MESH,
    )
    pair.start()

    spread(0)

    def fold(s):
        for i in SIDES:
            grad_row(s, i).wait_recv()
        for j in (-1, 1, 0):
            for m in range(3):
                whole = gsend[s, place(0, j), m]
                for i in SIDES:
                    keep = (r + i >= 0) & (r + i < rows)
                    whole = whole + jnp.where(keep, grow[s, i + 1, j + 1, m], 0.0)
                gsend[s, place(0, j), m] = whole
            if j != 0:
                grad_col(s, j).start()

    pair.wait_recv()
    half_in[...] = half_in[...] + pack[pl.ds(mine, HALF)]

    def plane_copy(q, sender):
        return pltpu.make_async_remote_copy(
            src_ref=half_in.at[pl.ds(q * share, share)],
            dst_ref=plane_in.at[sender],
            send_sem=plane_s.at[q],
            recv_sem=plane_r.at[sender],
            device_id=in_plane(q),
            device_id_type=MESH,
        )

    for q in range(owners):
        @pl.when(me != q)
        def _():
            plane_copy(q, me).start()

    fold(1)
    for i in SIDES:
        grad_row(0, i).start()

    def update(s):
        for j in SIDES:
            grad_col(s, j).wait_recv()
        sums = []
        for m in range(3):
            whole = gsend[s, place(0, 0), m]
            for j in SIDES:
                keep = (c + j >= 0) & (c + j < cols)
                whole = whole + jnp.where(keep, gcol[s, j + 1, m], 0.0)
            sums.append(whole)
        for p, part in enumerate(unpacked(*sums)):
            k, at = p // 2, pl.ds(p % 2 * PART, PART)
            obj_out[s, k, at] = obj[s, k, at] - OBJECT_RATE * part[:, :TILE]

    my_share = pl.multiple_of(me * share, 8)

    def deep_copy(k, sender):
        return pltpu.make_async_remote_copy(
            src_ref=deep_in.at[z],
            dst_ref=deep_in.at[sender],
            send_sem=deep_s.at[k],
            recv_sem=deep_r.at[sender],
            device_id=in_depth(k),
            device_id_type=MESH,
        )

    @pl.when(me < owners)
    def _():
        whole = half_in[pl.ds(my_share, share)]
        for p in range(group):
            @pl.when(me != p)
            def _():
                plane_copy(0, p).wait_recv()
        plane_in[me] = whole
        whole = plane_in[0]
        for p in range(1, group):
            whole = whole + plane_in[p]
        deep_in[z] = whole
        for k in range(depth):
            @pl.when(z != k)
            def _():
                deep_copy(k, z).start()

    fold(0)
    update(1)

    def back_copy(p, sender):
        at = pl.ds(pl.multiple_of(mine + sender * share, 8), share)
        return pltpu.make_async_remote_copy(
            src_ref=total.at[at],
            dst_ref=total.at[at],
            send_sem=back_s.at[p],
            recv_sem=back_r.at[sender],
            device_id=in_plane(p),
            device_id_type=MESH,
        )

    def last_copy(base, q):
        at = pl.ds(pl.multiple_of(base + q * share, 8), share)
        return pltpu.make_async_remote_copy(
            src_ref=total.at[at],
            dst_ref=total.at[at],
            send_sem=last_s.at[q],
            recv_sem=last_r.at[q],
            device_id=other,
            device_id_type=MESH,
        )

    @pl.when(me < owners)
    def _():
        for k in range(depth):
            @pl.when(z != k)
            def _():
                deep_copy(0, k).wait_recv()
        whole = deep_in[0]
        for k in range(1, depth):
            whole = whole + deep_in[k]
        total[pl.ds(pl.multiple_of(mine + my_share, 8), share)] = whole
        for p in range(group):
            @pl.when(me != p)
            def _():
                back_copy(p, me).start()

    update(0)

    for q in range(owners):
        @pl.when(me != q)
        def _():
            back_copy(0, q).wait_recv()
        last_copy(mine, q).start()
    for q in range(owners):
        last_copy(theirs, q).wait_recv()

    rate = PROBE_RATE / (SLOTS * rows * cols)

    def finish(at):
        d = pl.ds(at, step)
        re = total[d]
        im = total[pl.ds(WIDTH + at, step)]
        rest = total[pl.ds(2 * WIDTH + at, step)]
        probe_out[0, d, :128] = probe[0, d, :128] - rate * re
        probe_out[1, d, :128] = probe[1, d, :128] - rate * im
        probe_out[0, d, 128:] = probe[0, d, 128:] - rate * rest[:, :64]
        probe_out[1, d, 128:] = probe[1, d, 128:] - rate * pltpu.roll(rest, 64, 1)[:, :64]

    chunks(finish, step)

    for i, j in AROUND:
        halo_copy(i, j).wait_send()
    for i in SIDES:
        col_copy(i).wait_send()
        row_copy(i).wait_send()
        for s in range(2):
            grad_row(s, i).wait_send()
            grad_col(s, i).wait_send()
    pair.wait_send()
    for q in range(owners):
        @pl.when(me != q)
        def _():
            plane_copy(q, me).wait_send()
        last_copy(mine, q).wait_send()

    @pl.when(me < owners)
    def _():
        for k in range(depth):
            @pl.when(z != k)
            def _():
                deep_copy(k, z).wait_send()
        for p in range(group):
            @pl.when(me != p)
            def _():
                back_copy(p, me).wait_send()


def solution(mesh):
    rows, cols = mesh.shape["row"], mesh.shape["col"]
    group, depth = 2 * cols, rows // 4
    share = -(-(HALF // 8) // group) * 8
    owners = HALF // share
    consts = matrices()

    def shards(object_slices, probe, propagator_phase, measured, offsets, counts):
        vmem = pl.BlockSpec(memory_space=pltpu.VMEM)
        dma = pltpu.SemaphoreType.DMA
        square = (WIDTH, LANES)
        return pl.pallas_call(
            functools.partial(kernel, rows, cols, share, owners),
            out_shape=(
                jax.ShapeDtypeStruct(object_slices.shape, F32),
                jax.ShapeDtypeStruct(probe.shape, F32),
            ),
            in_specs=[pl.BlockSpec(memory_space=pltpu.HBM)] * 9,
            out_specs=(vmem, vmem),
            scratch_shapes=[
                pltpu.SMEM((1, 1, SLOTS, 2), jnp.int32),
                pltpu.SMEM((1, 1), jnp.int32),
                pltpu.VMEM(object_slices.shape, F32),
                pltpu.VMEM(probe.shape, F32),
                pltpu.VMEM(propagator_phase.shape, F32),
                pltpu.VMEM(measured.shape[2:], F32),
                *[pltpu.VMEM(m.shape, BF16) for m in consts],
                dma((9,)),
                pltpu.VMEM((2, 2, TILE, 128), F32),
                pltpu.VMEM((2, 9, 3, PART, 128), F32),
                pltpu.VMEM((2, 3, 3 * TILE, 128), F32),
                pltpu.VMEM((2, SLOTS, 2) + square, F32),
                pltpu.VMEM((2,) + square, F32),
                pltpu.VMEM((2,) + square, F32),
                pltpu.VMEM((SLOTS * WIDTH, 2 * LANES), BF16),
                pltpu.VMEM((SLOTS * WIDTH, 2 * LANES), BF16),
                pltpu.VMEM((SLOTS, 6 * WIDTH, LANES), BF16),
                pltpu.VMEM((SLOTS, 2 * WIDTH, LANES), F32),
                pltpu.VMEM((SLOTS, 2) + square, F32),
                pltpu.VMEM((SLOTS, 2, 2, 4 * TILE, 128), F32),
                pltpu.VMEM((2, 9, 3, PART, 128), F32),
                pltpu.VMEM((2, 3, 3, 3, PART, 128), F32),
                pltpu.VMEM((2, 3, 3, PART, 128), F32),
                pltpu.VMEM((2 * HALF, 128), F32),
                pltpu.VMEM((HALF, 128), F32),
                pltpu.VMEM((group, share, 128), F32),
                pltpu.VMEM((depth, share, 128), F32),
                pltpu.VMEM((2 * HALF, 128), F32),
                dma((9,)), dma((9,)),
                dma((3,)), dma((3,)), dma((3,)), dma((3,)),
                dma((2, 3)), dma((2, 3)), dma((2, 3)), dma((2, 3)),
                dma, dma,
                dma((owners,)), dma((group,)),
                dma((depth,)), dma((depth,)),
                dma((group,)), dma((owners,)),
                dma((owners,)), dma((owners,)),
            ],
            compiler_params=pltpu.CompilerParams(
                collective_id=0, has_side_effects=True, vmem_limit_bytes=48 * 1024 * 1024
            ),
        )(
            pltpu.with_memory_space_constraint(offsets, pltpu.HBM), counts,
            *[
                pltpu.with_memory_space_constraint(x, pltpu.HBM)
                for x in (object_slices, probe, propagator_phase, measured)
            ],
            *[pltpu.with_memory_space_constraint(jnp.asarray(m), pltpu.HBM) for m in consts],
        )

    return jax.shard_map(
        shards,
        mesh=mesh,
        in_specs=(
            P(None, None, "row", "col"),
            P(),
            P(),
            P("row", "col", None, None, None),
            P("row", "col", None, None),
            P("row", "col"),
        ),
        out_specs=(P(None, None, "row", "col"), P()),
        check_vma=False,
    )
```

```python
import functools

import jax
import jax.numpy as jnp
import ml_dtypes
import numpy as np
from jax import lax
from jax.experimental import pallas as pl
from jax.experimental.pallas import tpu as pltpu
from jax.sharding import PartitionSpec as P

OBJECT_RATE = 0.02
PROBE_RATE = 0.3
TILE = 96
WIDTH = 192
LANES = 256
SLOTS = 2
HALF = 288
PART = 48
MESH = pl.DeviceIdType.MESH
SIDES = (-1, 1)
AROUND = [(-1, -1), (-1, 1), (1, -1), (1, 1), (0, -1), (0, 1), (-1, 0), (1, 0)]
F32 = jnp.float32
BF16 = jnp.bfloat16


def place(i, j):
    return (i + 1) * 3 + (j + 1)


def matrices():
    n = np.arange(WIDTH)
    angle = 2.0 * np.pi * (np.outer(n, n) % WIDTH) / WIDTH
    c = np.cos(angle) / np.sqrt(WIDTH)
    s = np.sin(angle) / np.sqrt(WIDTH)
    right = np.zeros((2 * LANES, 2 * LANES))
    right[:WIDTH, :WIDTH] = c
    right[:WIDTH, LANES : LANES + WIDTH] = -s
    right[LANES : LANES + WIDTH, :WIDTH] = s
    right[LANES : LANES + WIDTH, LANES : LANES + WIDTH] = c
    left = np.block([[c, s], [-s, c]])
    parts = []
    for full in (right, left):
        high = full.astype(np.float32).astype(ml_dtypes.bfloat16)
        low = (full - high.astype(np.float64)).astype(np.float32).astype(ml_dtypes.bfloat16)
        parts += [high, low]
    return parts[:2] + [np.concatenate([parts[2], parts[2], parts[3]], axis=1)]


def two(x):
    high = x.astype(BF16)
    return high, (x - high.astype(F32)).astype(BF16)


def times(ar, ai, br, bi):
    return ar * br - ai * bi, ar * bi + ai * br


def times_conj(ar, ai, br, bi):
    return ar * br + ai * bi, ar * bi - ai * br


def packed(a, b, c, d):
    lane = lax.broadcasted_iota(jnp.int32, a.shape, 1)
    b, c, d = pltpu.roll(b, 96, 1), pltpu.roll(c, 64, 1), pltpu.roll(d, 32, 1)
    return jnp.where(lane < 96, a, b), jnp.where(lane < 64, b, c), jnp.where(lane < 32, c, d)


def unpacked(u, v, w):
    lane = lax.broadcasted_iota(jnp.int32, u.shape, 1)
    b = jnp.where(lane < 32, pltpu.roll(u, 32, 1), pltpu.roll(v, 32, 1))
    c = jnp.where(lane < 64, pltpu.roll(v, 64, 1), pltpu.roll(w, 64, 1))
    return u, b, c, pltpu.roll(w, 96, 1)


def dot(a, b):
    return jnp.dot(a, b, preferred_element_type=F32)


def chunks(body, step, total=WIDTH):
    for at in range(0, total, step):
        body(at)


def kernel(
    rows, cols, share, owners,
    offsets_in, counts_in, obj_in, probe_in, phase_in, measured_in, *rest,
):
    wide_in, (obj_out, probe_out), rest = rest[:3], rest[3:5], rest[5:]
    fetch(rows, cols, share, owners, offsets_in, counts_in, obj_in, probe_in, phase_in,
          measured_in, wide_in, obj_out, probe_out, *rest)


def fetch(
    rows, cols, share, owners,
    offsets_in, counts_in, obj_in, probe_in, phase_in, measured_in, wide_in,
    obj_out, probe_out,
    offsets, counts, obj, probe, phase, measured, wrh, wrl, wl, load,
    wide, halo, band, win, wave, trans, xh, xl, lh, y, carried, shift,
    gsend, grow, gcol, pack, half_in, plane_in, deep_in, total,
    halo_s, halo_r, col_s, col_r, row_s, row_r, grow_s, grow_r, gcol_s, gcol_r, pair_s, pair_r, plane_s, plane_r, deep_s, deep_r,
    back_s, back_r, last_s, last_r,
):
    r = lax.axis_index("row")
    c = lax.axis_index("col")
    core = lax.rem(r, 2)
    x_lo = lax.rem(lax.div(r, 2), 2)
    z = lax.div(r, 4)
    depth = rows // 4
    group = 2 * cols
    me = x_lo * cols + c
    other = (r + 1 - 2 * core, c)

    def beside(i, j):
        return (lax.rem(r + i + rows, rows), lax.rem(c + j + cols, cols))

    def in_plane(p):
        return (z * 4 + (p // cols) * 2 + core, p % cols)

    def in_depth(k):
        return (k * 4 + x_lo * 2 + core, c)

    def inside(i, j):
        return (r + i >= 0) & (r + i < rows) & (c + j >= 0) & (c + j < cols)

    loads = [
        pltpu.make_async_copy(a, b, load.at[i])
        for i, (a, b) in enumerate(
            zip(
                (obj_in, offsets_in, counts_in, probe_in, phase_in, *wide_in, measured_in.at[0, 0]),
                (obj, offsets, counts, probe, phase, wrh, wrl, wl, measured),
            )
        )
    ]
    for one in loads:
        one.start()

    barrier = pltpu.get_barrier_semaphore()

    def greet(device):
        pl.semaphore_signal(barrier, inc=1, device_id=device, device_id_type=MESH)

    for i, j in AROUND:
        greet(beside(i, j))
    greet(other)
    for d in range(1, group):
        p = lax.rem(me + d, group)
        greet((z * 4 + lax.div(p, cols) * 2 + core, lax.rem(p, cols)))
    for d in range(1, depth):
        greet((lax.rem(z + d, depth) * 4 + x_lo * 2 + core, c))

    loads[0].wait()
    for s in range(2):
        quarters = []
        for k in range(2):
            wide[s, k] = jnp.zeros((TILE, 128), F32)
            wide[s, k, :, :TILE] = obj[s, k]
            quarters += [wide[s, k, :PART], wide[s, k, PART:]]
        for m, v in enumerate(packed(*quarters)):
            halo[s, place(0, 0), m] = v

    pl.semaphore_wait(barrier, len(AROUND) + group + depth - 1)

    def halo_copy(i, j):
        return pltpu.make_async_remote_copy(
            src_ref=halo.at[0, place(0, 0)],
            dst_ref=halo.at[0, place(-i, -j)],
            send_sem=halo_s.at[place(i, j)],
            recv_sem=halo_r.at[place(-i, -j)],
            device_id=beside(i, j),
            device_id_type=MESH,
        )

    def col_copy(j):
        return pltpu.make_async_remote_copy(
            src_ref=halo.at[1, place(0, 0)],
            dst_ref=halo.at[1, place(0, -j)],
            send_sem=col_s.at[j + 1],
            recv_sem=col_r.at[1 - j],
            device_id=beside(0, j),
            device_id_type=MESH,
        )

    def row_copy(i):
        return pltpu.make_async_remote_copy(
            src_ref=halo.at[1, pl.ds(place(0, -1), 3)],
            dst_ref=halo.at[1, pl.ds(place(-i, -1), 3)],
            send_sem=row_s.at[i + 1],
            recv_sem=row_r.at[1 - i],
            device_id=beside(i, 0),
            device_id_type=MESH,
        )

    def grad_row(s, i):
        return pltpu.make_async_remote_copy(
            src_ref=gsend.at[s, pl.ds(place(i, -1), 3)],
            dst_ref=grow.at[s, 1 - i],
            send_sem=grow_s.at[s, i + 1],
            recv_sem=grow_r.at[s, 1 - i],
            device_id=beside(i, 0),
            device_id_type=MESH,
        )

    def grad_col(s, j):
        return pltpu.make_async_remote_copy(
            src_ref=gsend.at[s, place(0, j)],
            dst_ref=gcol.at[s, 1 - j],
            send_sem=gcol_s.at[s, j + 1],
            recv_sem=gcol_r.at[s, 1 - j],
            device_id=beside(0, j),
            device_id_type=MESH,
        )

    for j in SIDES:
        col_copy(j).start()
    for i, j in AROUND:
        halo_copy(i, j).start()

    for one in loads[1:]:
        one.wait()
    for k in range(2):
        wave[k] = jnp.zeros((WIDTH, LANES), F32)
        wave[k, :, :WIDTH] = probe[k]
        trans[k] = jnp.zeros((WIDTH, LANES), F32)
    trans[0, :, :WIDTH] = jnp.cos(phase[...])
    trans[1, :, :WIDTH] = jnp.sin(phase[...])
    for slot in range(SLOTS):
        for k in range(2):
            for m in range(2):
                shift[slot, k, m, :TILE] = jnp.zeros((TILE, 128), F32)
                shift[slot, k, m, TILE + WIDTH :] = jnp.zeros((TILE, 128), F32)

    ro = [offsets[0, 0, slot, 0] for slot in range(SLOTS)]
    co = [offsets[0, 0, slot, 1] for slot in range(SLOTS)]
    live = [slot < counts[0, 0] for slot in range(SLOTS)]

    def windows(s):
        lane = lax.broadcasted_iota(jnp.int32, (PART, 128), 1)
        for i in (-1, 0, 1):
            tiles = []
            for j in (-1, 0, 1):
                if (i, j) == (0, 0):
                    tiles.append(unpacked(*[halo[s, place(0, 0), m] for m in range(3)]))
                else:
                    keep = inside(i, j)
                    tiles.append(
                        unpacked(
                            *[jnp.where(keep, halo[s, place(i, j), m], 0.0) for m in range(3)]
                        )
                    )
            for k in range(2):
                for h in range(2):
                    a, b, d = [tile[2 * k + h] for tile in tiles]
                    b = pltpu.roll(b, 96, 1)
                    d = pltpu.roll(d, 64, 1)
                    at = pl.ds((i + 1) * TILE + h * PART, PART)
                    band[k, 0, at] = jnp.where(lane < 96, a, b)
                    band[k, 1, at] = jnp.where(lane < 64, b, d)
                    band[k, 2, at] = jnp.where(lane < 64, d, 0.0)
        for slot in range(SLOTS):
            for k in range(2):
                lane = lax.broadcasted_iota(jnp.int32, (WIDTH, 128), 1)
                turn = lax.rem(128 - co[slot], 128)
                at = pl.ds(ro[slot], WIDTH)
                v = [pltpu.roll(band[k, m, at], turn, 1) for m in range(3)]
                keep = lane < 128 - co[slot]
                win[s, slot, k, :, 0:128] = jnp.where(keep, v[0], v[1])
                win[s, slot, k, :, 128:256] = jnp.where(keep, v[1], v[2])

    def put(slot, at, step, re, im, inverse):
        if inverse:
            re, im = im, re
        to = pl.ds(slot * WIDTH + at, step)
        xh[to, :LANES], xl[to, :LANES] = two(re)
        xh[to, LANES:], xl[to, LANES:] = two(im)

    def transform():
        acc = dot(xh[...], wrh[...]) + dot(xl[...], wrh[...]) + dot(xh[...], wrl[...])
        for slot in range(SLOTS):
            part = acc[slot * WIDTH : (slot + 1) * WIDTH]
            for k in range(2):
                high, low = two(part[:, k * LANES : (k + 1) * LANES])
                for m, piece in enumerate((high, low, high)):
                    at = 2 * m * WIDTH + k * WIDTH
                    lh[slot, at : at + WIDTH] = piece
        for slot in range(SLOTS):
            y[slot] = dot(wl[...], lh[slot])

    def got(slot, at, step, inverse):
        one = y[slot, pl.ds(at, step), :]
        two_ = y[slot, pl.ds(WIDTH + at, step), :]
        return (two_, one) if inverse else (one, two_)

    step = 32

    def each(body):
        for slot in range(SLOTS):
            chunks(functools.partial(body, slot), step)

    def spread(s):
        lane = lax.broadcasted_iota(jnp.int32, (PART, 128), 1)
        for i in (-1, 0, 1):
            tiles = ([], [], [])
            for k in range(2):
                for h in range(2):
                    v = [0.0, 0.0, 0.0]
                    for slot in range(SLOTS):
                        at = pl.ds(TILE * (i + 2) + PART * h - ro[slot], PART)
                        a = pltpu.roll(shift[slot, k, 0, at], co[slot], 1)
                        b = pltpu.roll(shift[slot, k, 1, at], co[slot], 1)
                        wrap = lane < co[slot]
                        v[0] = v[0] + jnp.where(wrap, 0.0, a)
                        v[1] = v[1] + jnp.where(wrap, a, b)
                        v[2] = v[2] + jnp.where(wrap, b, 0.0)
                    tiles[0].append(v[0])
                    tiles[1].append(
                        jnp.where(lane < 32, pltpu.roll(v[0], 32, 1), pltpu.roll(v[1], 32, 1))
                    )
                    tiles[2].append(
                        jnp.where(lane < 64, pltpu.roll(v[1], 64, 1), pltpu.roll(v[2], 64, 1))
                    )
            for j in (-1, 0, 1):
                for m, part in enumerate(packed(*tiles[j + 1])):
                    gsend[s, place(i, j), m] = part

    def shifted(slot, at, re, im):
        to = pl.ds(TILE + at, step)
        for k, part in enumerate((re, im)):
            part = jnp.where(live[slot], part, 0.0)
            shift[slot, k, 0, to] = part[:, :128]
            shift[slot, k, 1, to] = part[:, 128:]

    for j in SIDES:
        col_copy(j).wait_recv()
    for i in SIDES:
        row_copy(i).start()
    for i, j in AROUND:
        halo_copy(i, j).wait_recv()
    windows(0)

    def enter(slot, at):
        d = pl.ds(at, step)
        re, im = times(wave[0, d], wave[1, d], win[0, slot, 0, d], win[0, slot, 1, d])
        put(slot, at, step, re, im, False)

    each(enter)
    transform()

    def carry(slot, at):
        d = pl.ds(at, step)
        re, im = got(slot, at, step, False)
        re, im = times(trans[0, d], trans[1, d], re, im)
        put(slot, at, step, re, im, True)

    each(carry)
    transform()

    for i in SIDES:
        row_copy(i).wait_recv()
    windows(1)

    def leave(slot, at):
        d = pl.ds(at, step)
        re, im = got(slot, at, step, True)
        carried[slot, 0, d] = re
        carried[slot, 1, d] = im
        re, im = times(re, im, win[1, slot, 0, d], win[1, slot, 1, d])
        put(slot, at, step, re, im, False)

    each(leave)
    transform()

    def residual(slot, at):
        re, im = got(slot, at, step, False)
        seen = jnp.concatenate(
            [measured[slot, pl.ds(at, step), :], jnp.zeros((step, LANES - WIDTH), F32)], axis=1
        )
        resid = re * re + im * im - seen
        put(slot, at, step, resid * re, resid * im, True)

    each(residual)
    transform()

    def second(slot, at):
        d = pl.ds(at, step)
        re, im = got(slot, at, step, True)
        shifted(slot, at, *times_conj(carried[slot, 0, d], carried[slot, 1, d], re, im))
        re, im = times_conj(win[1, slot, 0, d], win[1, slot, 1, d], re, im)
        put(slot, at, step, re, im, False)

    each(second)
    spread(1)
    for i in SIDES:
        grad_row(1, i).start()
    transform()

    def inner(slot, at):
        d = pl.ds(at, step)
        re, im = got(slot, at, step, False)
        re, im = times_conj(trans[0, d], trans[1, d], re, im)
        put(slot, at, step, re, im, True)

    each(inner)
    transform()

    def probe_part(at):
        d = pl.ds(at, step)
        re = jnp.zeros((step, LANES), F32)
        im = jnp.zeros((step, LANES), F32)
        for slot in range(SLOTS):
            ir, ii = got(slot, at, step, True)
            pr, pi = times_conj(win[0, slot, 0, d], win[0, slot, 1, d], ir, ii)
            re = re + jnp.where(live[slot], pr, 0.0)
            im = im + jnp.where(live[slot], pi, 0.0)
        lane = lax.broadcasted_iota(jnp.int32, (step, 128), 1)
        pack[d] = re[:, :128]
        pack[pl.ds(WIDTH + at, step)] = im[:, :128]
        pack[pl.ds(2 * WIDTH + at, step)] = jnp.where(
            lane < 64, re[:, 128:], pltpu.roll(im[:, 128:], 64, 1)
        )

    chunks(probe_part, step)

    mine = pl.multiple_of(HALF * core, 8)
    theirs = pl.multiple_of(HALF * (1 - core), 8)
    pair = pltpu.make_async_remote_copy(
        src_ref=pack.at[pl.ds(theirs, HALF)],
        dst_ref=half_in,
        send_sem=pair_s,
        recv_sem=pair_r,
        device_id=other,
        device_id_type=MESH,
    )
    pair.start()

    def first(slot, at):
        d = pl.ds(at, step)
        shifted(slot, at, *times_conj(wave[0, d], wave[1, d], *got(slot, at, step, True)))

    each(first)

    def fold(s):
        for i in SIDES:
            grad_row(s, i).wait_recv()
        for j in (-1, 1, 0):
            for m in range(3):
                whole = gsend[s, place(0, j), m]
                for i in SIDES:
                    keep = (r + i >= 0) & (r + i < rows)
                    whole = whole + jnp.where(keep, grow[s, i + 1, j + 1, m], 0.0)
                gsend[s, place(0, j), m] = whole
            if j != 0:
                grad_col(s, j).start()

    pair.wait_recv()
    half_in[...] = half_in[...] + pack[pl.ds(mine, HALF)]

    def plane_copy(q, sender):
        return pltpu.make_async_remote_copy(
            src_ref=half_in.at[pl.ds(q * share, share)],
            dst_ref=plane_in.at[sender],
            send_sem=plane_s.at[q],
            recv_sem=plane_r.at[sender],
            device_id=in_plane(q),
            device_id_type=MESH,
        )

    for q in range(owners):
        @pl.when(me != q)
        def _():
            plane_copy(q, me).start()

    spread(0)
    fold(1)
    for i in SIDES:
        grad_row(0, i).start()

    def update(s):
        for j in SIDES:
            grad_col(s, j).wait_recv()
        sums = []
        for m in range(3):
            whole = gsend[s, place(0, 0), m]
            for j in SIDES:
                keep = (c + j >= 0) & (c + j < cols)
                whole = whole + jnp.where(keep, gcol[s, j + 1, m], 0.0)
            sums.append(whole)
        for p, part in enumerate(unpacked(*sums)):
            k, at = p // 2, pl.ds(p % 2 * PART, PART)
            obj_out[s, k, at] = obj[s, k, at] - OBJECT_RATE * part[:, :TILE]

    my_share = pl.multiple_of(me * share, 8)

    def deep_copy(k, sender):
        return pltpu.make_async_remote_copy(
            src_ref=deep_in.at[z],
            dst_ref=deep_in.at[sender],
            send_sem=deep_s.at[k],
            recv_sem=deep_r.at[sender],
            device_id=in_depth(k),
            device_id_type=MESH,
        )

    @pl.when(me < owners)
    def _():
        whole = half_in[pl.ds(my_share, share)]
        for p in range(group):
            @pl.when(me != p)
            def _():
                plane_copy(0, p).wait_recv()
        plane_in[me] = whole
        whole = plane_in[0]
        for p in range(1, group):
            whole = whole + plane_in[p]
        deep_in[z] = whole
        for k in range(depth):
            @pl.when(z != k)
            def _():
                deep_copy(k, z).start()

    fold(0)
    update(1)

    def back_copy(p, sender):
        at = pl.ds(pl.multiple_of(mine + sender * share, 8), share)
        return pltpu.make_async_remote_copy(
            src_ref=total.at[at],
            dst_ref=total.at[at],
            send_sem=back_s.at[p],
            recv_sem=back_r.at[sender],
            device_id=in_plane(p),
            device_id_type=MESH,
        )

    def last_copy(base, q):
        at = pl.ds(pl.multiple_of(base + q * share, 8), share)
        return pltpu.make_async_remote_copy(
            src_ref=total.at[at],
            dst_ref=total.at[at],
            send_sem=last_s.at[q],
            recv_sem=last_r.at[q],
            device_id=other,
            device_id_type=MESH,
        )

    @pl.when(me < owners)
    def _():
        for k in range(depth):
            @pl.when(z != k)
            def _():
                deep_copy(0, k).wait_recv()
        whole = deep_in[0]
        for k in range(1, depth):
            whole = whole + deep_in[k]
        total[pl.ds(pl.multiple_of(mine + my_share, 8), share)] = whole
        for p in range(group):
            @pl.when(me != p)
            def _():
                back_copy(p, me).start()

    update(0)

    for q in range(owners):
        @pl.when(me != q)
        def _():
            back_copy(0, q).wait_recv()
        last_copy(mine, q).start()
    for q in range(owners):
        last_copy(theirs, q).wait_recv()

    rate = PROBE_RATE / (SLOTS * rows * cols)

    def finish(at):
        d = pl.ds(at, step)
        re = total[d]
        im = total[pl.ds(WIDTH + at, step)]
        rest = total[pl.ds(2 * WIDTH + at, step)]
        probe_out[0, d, :128] = probe[0, d, :128] - rate * re
        probe_out[1, d, :128] = probe[1, d, :128] - rate * im
        probe_out[0, d, 128:] = probe[0, d, 128:] - rate * rest[:, :64]
        probe_out[1, d, 128:] = probe[1, d, 128:] - rate * pltpu.roll(rest, 64, 1)[:, :64]

    chunks(finish, step)

    for i, j in AROUND:
        halo_copy(i, j).wait_send()
    for i in SIDES:
        col_copy(i).wait_send()
        row_copy(i).wait_send()
        for s in range(2):
            grad_row(s, i).wait_send()
            grad_col(s, i).wait_send()
    pair.wait_send()
    for q in range(owners):
        @pl.when(me != q)
        def _():
            plane_copy(q, me).wait_send()
        last_copy(mine, q).wait_send()

    @pl.when(me < owners)
    def _():
        for k in range(depth):
            @pl.when(z != k)
            def _():
                deep_copy(k, z).wait_send()
        for p in range(group):
            @pl.when(me != p)
            def _():
                back_copy(p, me).wait_send()


def solution(mesh):
    rows, cols = mesh.shape["row"], mesh.shape["col"]
    group, depth = 2 * cols, rows // 4
    share = -(-(HALF // 8) // group) * 8
    owners = HALF // share
    consts = matrices()

    def shards(object_slices, probe, propagator_phase, measured, offsets, counts):
        vmem = pl.BlockSpec(memory_space=pltpu.VMEM)
        dma = pltpu.SemaphoreType.DMA
        square = (WIDTH, LANES)
        return pl.pallas_call(
            functools.partial(kernel, rows, cols, share, owners),
            out_shape=(
                jax.ShapeDtypeStruct(object_slices.shape, F32),
                jax.ShapeDtypeStruct(probe.shape, F32),
            ),
            in_specs=[pl.BlockSpec(memory_space=pltpu.HBM)] * 9,
            out_specs=(vmem, vmem),
            scratch_shapes=[
                pltpu.SMEM((1, 1, SLOTS, 2), jnp.int32),
                pltpu.SMEM((1, 1), jnp.int32),
                pltpu.VMEM(object_slices.shape, F32),
                pltpu.VMEM(probe.shape, F32),
                pltpu.VMEM(propagator_phase.shape, F32),
                pltpu.VMEM(measured.shape[2:], F32),
                *[pltpu.VMEM(m.shape, BF16) for m in consts],
                dma((9,)),
                pltpu.VMEM((2, 2, TILE, 128), F32),
                pltpu.VMEM((2, 9, 3, PART, 128), F32),
                pltpu.VMEM((2, 3, 3 * TILE, 128), F32),
                pltpu.VMEM((2, SLOTS, 2) + square, F32),
                pltpu.VMEM((2,) + square, F32),
                pltpu.VMEM((2,) + square, F32),
                pltpu.VMEM((SLOTS * WIDTH, 2 * LANES), BF16),
                pltpu.VMEM((SLOTS * WIDTH, 2 * LANES), BF16),
                pltpu.VMEM((SLOTS, 6 * WIDTH, LANES), BF16),
                pltpu.VMEM((SLOTS, 2 * WIDTH, LANES), F32),
                pltpu.VMEM((SLOTS, 2) + square, F32),
                pltpu.VMEM((SLOTS, 2, 2, 4 * TILE, 128), F32),
                pltpu.VMEM((2, 9, 3, PART, 128), F32),
                pltpu.VMEM((2, 3, 3, 3, PART, 128), F32),
                pltpu.VMEM((2, 3, 3, PART, 128), F32),
                pltpu.VMEM((2 * HALF, 128), F32),
                pltpu.VMEM((HALF, 128), F32),
                pltpu.VMEM((group, share, 128), F32),
                pltpu.VMEM((depth, share, 128), F32),
                pltpu.VMEM((2 * HALF, 128), F32),
                dma((9,)), dma((9,)),
                dma((3,)), dma((3,)), dma((3,)), dma((3,)),
                dma((2, 3)), dma((2, 3)), dma((2, 3)), dma((2, 3)),
                dma, dma,
                dma((owners,)), dma((group,)),
                dma((depth,)), dma((depth,)),
                dma((group,)), dma((owners,)),
                dma((owners,)), dma((owners,)),
            ],
            compiler_params=pltpu.CompilerParams(
                collective_id=0, has_side_effects=True, vmem_limit_bytes=48 * 1024 * 1024
            ),
        )(
            pltpu.with_memory_space_constraint(offsets, pltpu.HBM), counts,
            *[
                pltpu.with_memory_space_constraint(x, pltpu.HBM)
                for x in (object_slices, probe, propagator_phase, measured)
            ],
            *[pltpu.with_memory_space_constraint(jnp.asarray(m), pltpu.HBM) for m in consts],
        )

    return jax.shard_map(
        shards,
        mesh=mesh,
        in_specs=(
            P(None, None, "row", "col"),
            P(),
            P(),
            P("row", "col", None, None, None),
            P("row", "col", None, None),
            P("row", "col"),
        ),
        out_specs=(P(None, None, "row", "col"), P()),
        check_vma=False,
    )
```

```python
import functools

import jax
import jax.numpy as jnp
import ml_dtypes
import numpy as np
from jax import lax
from jax.experimental import pallas as pl
from jax.experimental.pallas import tpu as pltpu
from jax.sharding import PartitionSpec as P

OBJECT_RATE = 0.02
PROBE_RATE = 0.3
TILE = 96
WIDTH = 192
LANES = 256
SLOTS = 2
HALF = 288
PART = 48
MESH = pl.DeviceIdType.MESH
SIDES = (-1, 1)
AROUND = [(-1, -1), (-1, 1), (1, -1), (1, 1), (0, -1), (0, 1), (-1, 0), (1, 0)]
F32 = jnp.float32
BF16 = jnp.bfloat16


def place(i, j):
    return (i + 1) * 3 + (j + 1)


def matrices():
    n = np.arange(WIDTH)
    angle = 2.0 * np.pi * (np.outer(n, n) % WIDTH) / WIDTH
    c = np.cos(angle) / np.sqrt(WIDTH)
    s = np.sin(angle) / np.sqrt(WIDTH)
    right = np.zeros((2 * LANES, 2 * LANES))
    right[:WIDTH, :WIDTH] = c
    right[:WIDTH, LANES : LANES + WIDTH] = -s
    right[LANES : LANES + WIDTH, :WIDTH] = s
    right[LANES : LANES + WIDTH, LANES : LANES + WIDTH] = c
    left = np.block([[c, s], [-s, c]])
    parts = []
    for full in (right, left):
        high = full.astype(np.float32).astype(ml_dtypes.bfloat16)
        low = (full - high.astype(np.float64)).astype(np.float32).astype(ml_dtypes.bfloat16)
        parts += [high, low]
    return parts[:2] + [np.concatenate([parts[2], parts[2], parts[3]], axis=1)]


def two(x):
    high = x.astype(BF16)
    return high, (x - high.astype(F32)).astype(BF16)


def times(ar, ai, br, bi):
    return ar * br - ai * bi, ar * bi + ai * br


def times_conj(ar, ai, br, bi):
    return ar * br + ai * bi, ar * bi - ai * br


def packed(a, b, c, d):
    lane = lax.broadcasted_iota(jnp.int32, a.shape, 1)
    b, c, d = pltpu.roll(b, 96, 1), pltpu.roll(c, 64, 1), pltpu.roll(d, 32, 1)
    return jnp.where(lane < 96, a, b), jnp.where(lane < 64, b, c), jnp.where(lane < 32, c, d)


def unpacked(u, v, w):
    lane = lax.broadcasted_iota(jnp.int32, u.shape, 1)
    b = jnp.where(lane < 32, pltpu.roll(u, 32, 1), pltpu.roll(v, 32, 1))
    c = jnp.where(lane < 64, pltpu.roll(v, 64, 1), pltpu.roll(w, 64, 1))
    return u, b, c, pltpu.roll(w, 96, 1)


def dot(a, b):
    return jnp.dot(a, b, preferred_element_type=F32)


def chunks(body, step, total=WIDTH):
    for at in range(0, total, step):
        body(at)


def kernel(
    rows, cols, share, owners,
    offsets_in, counts_in, obj_in, probe_in, phase_in, measured_in, *rest,
):
    wide_in, (obj_out, probe_out), rest = rest[:3], rest[3:5], rest[5:]
    fetch(rows, cols, share, owners, offsets_in, counts_in, obj_in, probe_in, phase_in,
          measured_in, wide_in, obj_out, probe_out, *rest)


def fetch(
    rows, cols, share, owners,
    offsets_in, counts_in, obj_in, probe_in, phase_in, measured_in, wide_in,
    obj_out, probe_out,
    offsets, counts, obj, probe, phase, measured, wrh, wrl, wl, load,
    wide, halo, band, win, wave, trans, xh, xl, lh, y, carried, shift,
    gsend, grow, gcol, pack, half_in, plane_in, deep_in, total,
    halo_s, halo_r, col_s, col_r, row_s, row_r, grow_s, grow_r, gcol_s, gcol_r, pair_s, pair_r, plane_s, plane_r, deep_s, deep_r,
    back_s, back_r, last_s, last_r,
):
    r = lax.axis_index("row")
    c = lax.axis_index("col")
    core = lax.rem(r, 2)
    x_lo = lax.rem(lax.div(r, 2), 2)
    z = lax.div(r, 4)
    depth = rows // 4
    group = 2 * cols
    me = x_lo * cols + c
    other = (r + 1 - 2 * core, c)

    def beside(i, j):
        return (lax.rem(r + i + rows, rows), lax.rem(c + j + cols, cols))

    def in_plane(p):
        return (z * 4 + (p // cols) * 2 + core, p % cols)

    def in_depth(k):
        return (k * 4 + x_lo * 2 + core, c)

    def inside(i, j):
        return (r + i >= 0) & (r + i < rows) & (c + j >= 0) & (c + j < cols)

    loads = [
        pltpu.make_async_copy(a, b, load.at[i])
        for i, (a, b) in enumerate(
            zip(
                (obj_in, offsets_in, counts_in, probe_in, phase_in, *wide_in, measured_in.at[0, 0]),
                (obj, offsets, counts, probe, phase, wrh, wrl, wl, measured),
            )
        )
    ]
    for one in loads:
        one.start()

    barrier = pltpu.get_barrier_semaphore()

    def greet(device):
        pl.semaphore_signal(barrier, inc=1, device_id=device, device_id_type=MESH)

    for i, j in AROUND:
        greet(beside(i, j))
    greet(other)
    for d in range(1, group):
        p = lax.rem(me + d, group)
        greet((z * 4 + lax.div(p, cols) * 2 + core, lax.rem(p, cols)))
    for d in range(1, depth):
        greet((lax.rem(z + d, depth) * 4 + x_lo * 2 + core, c))

    loads[0].wait()
    for s in range(2):
        quarters = []
        for k in range(2):
            wide[s, k] = jnp.zeros((TILE, 128), F32)
            wide[s, k, :, :TILE] = obj[s, k]
            quarters += [wide[s, k, :PART], wide[s, k, PART:]]
        for m, v in enumerate(packed(*quarters)):
            halo[s, place(0, 0), m] = v

    pl.semaphore_wait(barrier, len(AROUND) + group + depth - 1)

    def halo_copy(i, j):
        return pltpu.make_async_remote_copy(
            src_ref=halo.at[0, place(0, 0)],
            dst_ref=halo.at[0, place(-i, -j)],
            send_sem=halo_s.at[place(i, j)],
            recv_sem=halo_r.at[place(-i, -j)],
            device_id=beside(i, j),
            device_id_type=MESH,
        )

    def col_copy(j):
        return pltpu.make_async_remote_copy(
            src_ref=halo.at[1, place(0, 0)],
            dst_ref=halo.at[1, place(0, -j)],
            send_sem=col_s.at[j + 1],
            recv_sem=col_r.at[1 - j],
            device_id=beside(0, j),
            device_id_type=MESH,
        )

    def row_copy(i):
        return pltpu.make_async_remote_copy(
            src_ref=halo.at[1, pl.ds(place(0, -1), 3)],
            dst_ref=halo.at[1, pl.ds(place(-i, -1), 3)],
            send_sem=row_s.at[i + 1],
            recv_sem=row_r.at[1 - i],
            device_id=beside(i, 0),
            device_id_type=MESH,
        )

    def grad_row(s, i):
        return pltpu.make_async_remote_copy(
            src_ref=gsend.at[s, pl.ds(place(i, -1), 3)],
            dst_ref=grow.at[s, 1 - i],
            send_sem=grow_s.at[s, i + 1],
            recv_sem=grow_r.at[s, 1 - i],
            device_id=beside(i, 0),
            device_id_type=MESH,
        )

    def grad_col(s, j):
        return pltpu.make_async_remote_copy(
            src_ref=gsend.at[s, place(0, j)],
            dst_ref=gcol.at[s, 1 - j],
            send_sem=gcol_s.at[s, j + 1],
            recv_sem=gcol_r.at[s, 1 - j],
            device_id=beside(0, j),
            device_id_type=MESH,
        )

    for j in SIDES:
        col_copy(j).start()
    for i, j in AROUND:
        halo_copy(i, j).start()

    for one in loads[1:]:
        one.wait()
    for k in range(2):
        wave[k] = jnp.zeros((WIDTH, LANES), F32)
        wave[k, :, :WIDTH] = probe[k]
        trans[k] = jnp.zeros((WIDTH, LANES), F32)
    trans[0, :, :WIDTH] = jnp.cos(phase[...])
    trans[1, :, :WIDTH] = jnp.sin(phase[...])
    for slot in range(SLOTS):
        for k in range(2):
            for m in range(2):
                shift[slot, k, m, :TILE] = jnp.zeros((TILE, 128), F32)
                shift[slot, k, m, TILE + WIDTH :] = jnp.zeros((TILE, 128), F32)

    ro = [offsets[0, 0, slot, 0] for slot in range(SLOTS)]
    co = [offsets[0, 0, slot, 1] for slot in range(SLOTS)]
    live = [slot < counts[0, 0] for slot in range(SLOTS)]

    def windows(s):
        lane = lax.broadcasted_iota(jnp.int32, (PART, 128), 1)
        for i in (-1, 0, 1):
            tiles = []
            for j in (-1, 0, 1):
                if (i, j) == (0, 0):
                    tiles.append(unpacked(*[halo[s, place(0, 0), m] for m in range(3)]))
                else:
                    keep = inside(i, j)
                    tiles.append(
                        unpacked(
                            *[jnp.where(keep, halo[s, place(i, j), m], 0.0) for m in range(3)]
                        )
                    )
            for k in range(2):
                for h in range(2):
                    a, b, d = [tile[2 * k + h] for tile in tiles]
                    b = pltpu.roll(b, 96, 1)
                    d = pltpu.roll(d, 64, 1)
                    at = pl.ds((i + 1) * TILE + h * PART, PART)
                    band[k, 0, at] = jnp.where(lane < 96, a, b)
                    band[k, 1, at] = jnp.where(lane < 64, b, d)
                    band[k, 2, at] = jnp.where(lane < 64, d, 0.0)
        for slot in range(SLOTS):
            for k in range(2):
                lane = lax.broadcasted_iota(jnp.int32, (WIDTH, 128), 1)
                turn = lax.rem(128 - co[slot], 128)
                at = pl.ds(ro[slot], WIDTH)
                v = [pltpu.roll(band[k, m, at], turn, 1) for m in range(3)]
                keep = lane < 128 - co[slot]
                win[s, slot, k, :, 0:128] = jnp.where(keep, v[0], v[1])
                win[s, slot, k, :, 128:256] = jnp.where(keep, v[1], v[2])

    def put(slot, at, step, re, im, inverse):
        if inverse:
            re, im = im, re
        to = pl.ds(slot * WIDTH + at, step)
        xh[to, :LANES], xl[to, :LANES] = two(re)
        xh[to, LANES:], xl[to, LANES:] = two(im)

    def transform():
        for slot in range(SLOTS):
            d = slice(slot * WIDTH, (slot + 1) * WIDTH)
            part = dot(xh[d], wrh[...]) + dot(xl[d], wrh[...]) + dot(xh[d], wrl[...])
            for k in range(2):
                high, low = two(part[:, k * LANES : (k + 1) * LANES])
                for m, piece in enumerate((high, low, high)):
                    at = 2 * m * WIDTH + k * WIDTH
                    lh[slot, at : at + WIDTH] = piece
        for slot in range(SLOTS):
            y[slot] = dot(wl[...], lh[slot])

    def got(slot, at, step, inverse):
        one = y[slot, pl.ds(at, step), :]
        two_ = y[slot, pl.ds(WIDTH + at, step), :]
        return (two_, one) if inverse else (one, two_)

    step = 32

    def each(body):
        for slot in range(SLOTS):
            chunks(functools.partial(body, slot), step)

    def spread(s):
        lane = lax.broadcasted_iota(jnp.int32, (PART, 128), 1)
        for i in (-1, 0, 1):
            tiles = ([], [], [])
            for k in range(2):
                for h in range(2):
                    v = [0.0, 0.0, 0.0]
                    for slot in range(SLOTS):
                        at = pl.ds(TILE * (i + 2) + PART * h - ro[slot], PART)
                        a = pltpu.roll(shift[slot, k, 0, at], co[slot], 1)
                        b = pltpu.roll(shift[slot, k, 1, at], co[slot], 1)
                        wrap = lane < co[slot]
                        v[0] = v[0] + jnp.where(wrap, 0.0, a)
                        v[1] = v[1] + jnp.where(wrap, a, b)
                        v[2] = v[2] + jnp.where(wrap, b, 0.0)
                    tiles[0].append(v[0])
                    tiles[1].append(
                        jnp.where(lane < 32, pltpu.roll(v[0], 32, 1), pltpu.roll(v[1], 32, 1))
                    )
                    tiles[2].append(
                        jnp.where(lane < 64, pltpu.roll(v[1], 64, 1), pltpu.roll(v[2], 64, 1))
                    )
            for j in (-1, 0, 1):
                for m, part in enumerate(packed(*tiles[j + 1])):
                    gsend[s, place(i, j), m] = part

    def shifted(slot, at, re, im):
        to = pl.ds(TILE + at, step)
        for k, part in enumerate((re, im)):
            part = jnp.where(live[slot], part, 0.0)
            shift[slot, k, 0, to] = part[:, :128]
            shift[slot, k, 1, to] = part[:, 128:]

    for j in SIDES:
        col_copy(j).wait_recv()
    for i in SIDES:
        row_copy(i).start()
    for i, j in AROUND:
        halo_copy(i, j).wait_recv()
    windows(0)

    def enter(slot, at):
        d = pl.ds(at, step)
        re, im = times(wave[0, d], wave[1, d], win[0, slot, 0, d], win[0, slot, 1, d])
        put(slot, at, step, re, im, False)

    each(enter)
    transform()

    def carry(slot, at):
        d = pl.ds(at, step)
        re, im = got(slot, at, step, False)
        re, im = times(trans[0, d], trans[1, d], re, im)
        put(slot, at, step, re, im, True)

    each(carry)
    transform()

    for i in SIDES:
        row_copy(i).wait_recv()
    windows(1)

    def leave(slot, at):
        d = pl.ds(at, step)
        re, im = got(slot, at, step, True)
        carried[slot, 0, d] = re
        carried[slot, 1, d] = im
        re, im = times(re, im, win[1, slot, 0, d], win[1, slot, 1, d])
        put(slot, at, step, re, im, False)

    each(leave)
    transform()

    def residual(slot, at):
        re, im = got(slot, at, step, False)
        seen = jnp.concatenate(
            [measured[slot, pl.ds(at, step), :], jnp.zeros((step, LANES - WIDTH), F32)], axis=1
        )
        resid = re * re + im * im - seen
        put(slot, at, step, resid * re, resid * im, True)

    each(residual)
    transform()

    def second(slot, at):
        d = pl.ds(at, step)
        re, im = got(slot, at, step, True)
        shifted(slot, at, *times_conj(carried[slot, 0, d], carried[slot, 1, d], re, im))
        re, im = times_conj(win[1, slot, 0, d], win[1, slot, 1, d], re, im)
        put(slot, at, step, re, im, False)

    each(second)
    spread(1)
    for i in SIDES:
        grad_row(1, i).start()
    transform()

    def inner(slot, at):
        d = pl.ds(at, step)
        re, im = got(slot, at, step, False)
        re, im = times_conj(trans[0, d], trans[1, d], re, im)
        put(slot, at, step, re, im, True)

    each(inner)
    transform()

    def probe_part(at):
        d = pl.ds(at, step)
        re = jnp.zeros((step, LANES), F32)
        im = jnp.zeros((step, LANES), F32)
        for slot in range(SLOTS):
            ir, ii = got(slot, at, step, True)
            pr, pi = times_conj(win[0, slot, 0, d], win[0, slot, 1, d], ir, ii)
            re = re + jnp.where(live[slot], pr, 0.0)
            im = im + jnp.where(live[slot], pi, 0.0)
        lane = lax.broadcasted_iota(jnp.int32, (step, 128), 1)
        pack[d] = re[:, :128]
        pack[pl.ds(WIDTH + at, step)] = im[:, :128]
        pack[pl.ds(2 * WIDTH + at, step)] = jnp.where(
            lane < 64, re[:, 128:], pltpu.roll(im[:, 128:], 64, 1)
        )

    chunks(probe_part, step)

    mine = pl.multiple_of(HALF * core, 8)
    theirs = pl.multiple_of(HALF * (1 - core), 8)
    pair = pltpu.make_async_remote_copy(
        src_ref=pack.at[pl.ds(theirs, HALF)],
        dst_ref=half_in,
        send_sem=pair_s,
        recv_sem=pair_r,
        device_id=other,
        device_id_type=MESH,
    )
    pair.start()

    def first(slot, at):
        d = pl.ds(at, step)
        shifted(slot, at, *times_conj(wave[0, d], wave[1, d], *got(slot, at, step, True)))

    each(first)

    def fold(s):
        for i in SIDES:
            grad_row(s, i).wait_recv()
        for j in (-1, 1, 0):
            for m in range(3):
                whole = gsend[s, place(0, j), m]
                for i in SIDES:
                    keep = (r + i >= 0) & (r + i < rows)
                    whole = whole + jnp.where(keep, grow[s, i + 1, j + 1, m], 0.0)
                gsend[s, place(0, j), m] = whole
            if j != 0:
                grad_col(s, j).start()

    pair.wait_recv()
    half_in[...] = half_in[...] + pack[pl.ds(mine, HALF)]

    def plane_copy(q, sender):
        return pltpu.make_async_remote_copy(
            src_ref=half_in.at[pl.ds(q * share, share)],
            dst_ref=plane_in.at[sender],
            send_sem=plane_s.at[q],
            recv_sem=plane_r.at[sender],
            device_id=in_plane(q),
            device_id_type=MESH,
        )

    for q in range(owners):
        @pl.when(me != q)
        def _():
            plane_copy(q, me).start()

    spread(0)
    fold(1)
    for i in SIDES:
        grad_row(0, i).start()

    def update(s):
        for j in SIDES:
            grad_col(s, j).wait_recv()
        sums = []
        for m in range(3):
            whole = gsend[s, place(0, 0), m]
            for j in SIDES:
                keep = (c + j >= 0) & (c + j < cols)
                whole = whole + jnp.where(keep, gcol[s, j + 1, m], 0.0)
            sums.append(whole)
        for p, part in enumerate(unpacked(*sums)):
            k, at = p // 2, pl.ds(p % 2 * PART, PART)
            obj_out[s, k, at] = obj[s, k, at] - OBJECT_RATE * part[:, :TILE]

    my_share = pl.multiple_of(me * share, 8)

    def deep_copy(k, sender):
        return pltpu.make_async_remote_copy(
            src_ref=deep_in.at[z],
            dst_ref=deep_in.at[sender],
            send_sem=deep_s.at[k],
            recv_sem=deep_r.at[sender],
            device_id=in_depth(k),
            device_id_type=MESH,
        )

    @pl.when(me < owners)
    def _():
        whole = half_in[pl.ds(my_share, share)]
        for p in range(group):
            @pl.when(me != p)
            def _():
                plane_copy(0, p).wait_recv()
        plane_in[me] = whole
        whole = plane_in[0]
        for p in range(1, group):
            whole = whole + plane_in[p]
        deep_in[z] = whole
        for k in range(depth):
            @pl.when(z != k)
            def _():
                deep_copy(k, z).start()

    fold(0)
    update(1)

    def back_copy(p, sender):
        at = pl.ds(pl.multiple_of(mine + sender * share, 8), share)
        return pltpu.make_async_remote_copy(
            src_ref=total.at[at],
            dst_ref=total.at[at],
            send_sem=back_s.at[p],
            recv_sem=back_r.at[sender],
            device_id=in_plane(p),
            device_id_type=MESH,
        )

    def last_copy(base, q):
        at = pl.ds(pl.multiple_of(base + q * share, 8), share)
        return pltpu.make_async_remote_copy(
            src_ref=total.at[at],
            dst_ref=total.at[at],
            send_sem=last_s.at[q],
            recv_sem=last_r.at[q],
            device_id=other,
            device_id_type=MESH,
        )

    @pl.when(me < owners)
    def _():
        for k in range(depth):
            @pl.when(z != k)
            def _():
                deep_copy(0, k).wait_recv()
        whole = deep_in[0]
        for k in range(1, depth):
            whole = whole + deep_in[k]
        total[pl.ds(pl.multiple_of(mine + my_share, 8), share)] = whole
        for p in range(group):
            @pl.when(me != p)
            def _():
                back_copy(p, me).start()

    update(0)

    for q in range(owners):
        @pl.when(me != q)
        def _():
            back_copy(0, q).wait_recv()
        last_copy(mine, q).start()
    for q in range(owners):
        last_copy(theirs, q).wait_recv()

    rate = PROBE_RATE / (SLOTS * rows * cols)

    def finish(at):
        d = pl.ds(at, step)
        re = total[d]
        im = total[pl.ds(WIDTH + at, step)]
        rest = total[pl.ds(2 * WIDTH + at, step)]
        probe_out[0, d, :128] = probe[0, d, :128] - rate * re
        probe_out[1, d, :128] = probe[1, d, :128] - rate * im
        probe_out[0, d, 128:] = probe[0, d, 128:] - rate * rest[:, :64]
        probe_out[1, d, 128:] = probe[1, d, 128:] - rate * pltpu.roll(rest, 64, 1)[:, :64]

    chunks(finish, step)

    for i, j in AROUND:
        halo_copy(i, j).wait_send()
    for i in SIDES:
        col_copy(i).wait_send()
        row_copy(i).wait_send()
        for s in range(2):
            grad_row(s, i).wait_send()
            grad_col(s, i).wait_send()
    pair.wait_send()
    for q in range(owners):
        @pl.when(me != q)
        def _():
            plane_copy(q, me).wait_send()
        last_copy(mine, q).wait_send()

    @pl.when(me < owners)
    def _():
        for k in range(depth):
            @pl.when(z != k)
            def _():
                deep_copy(k, z).wait_send()
        for p in range(group):
            @pl.when(me != p)
            def _():
                back_copy(p, me).wait_send()


def solution(mesh):
    rows, cols = mesh.shape["row"], mesh.shape["col"]
    group, depth = 2 * cols, rows // 4
    share = -(-(HALF // 8) // group) * 8
    owners = HALF // share
    consts = matrices()

    def shards(object_slices, probe, propagator_phase, measured, offsets, counts):
        vmem = pl.BlockSpec(memory_space=pltpu.VMEM)
        dma = pltpu.SemaphoreType.DMA
        square = (WIDTH, LANES)
        return pl.pallas_call(
            functools.partial(kernel, rows, cols, share, owners),
            out_shape=(
                jax.ShapeDtypeStruct(object_slices.shape, F32),
                jax.ShapeDtypeStruct(probe.shape, F32),
            ),
            in_specs=[pl.BlockSpec(memory_space=pltpu.HBM)] * 9,
            out_specs=(vmem, vmem),
            scratch_shapes=[
                pltpu.SMEM((1, 1, SLOTS, 2), jnp.int32),
                pltpu.SMEM((1, 1), jnp.int32),
                pltpu.VMEM(object_slices.shape, F32),
                pltpu.VMEM(probe.shape, F32),
                pltpu.VMEM(propagator_phase.shape, F32),
                pltpu.VMEM(measured.shape[2:], F32),
                *[pltpu.VMEM(m.shape, BF16) for m in consts],
                dma((9,)),
                pltpu.VMEM((2, 2, TILE, 128), F32),
                pltpu.VMEM((2, 9, 3, PART, 128), F32),
                pltpu.VMEM((2, 3, 3 * TILE, 128), F32),
                pltpu.VMEM((2, SLOTS, 2) + square, F32),
                pltpu.VMEM((2,) + square, F32),
                pltpu.VMEM((2,) + square, F32),
                pltpu.VMEM((SLOTS * WIDTH, 2 * LANES), BF16),
                pltpu.VMEM((SLOTS * WIDTH, 2 * LANES), BF16),
                pltpu.VMEM((SLOTS, 6 * WIDTH, LANES), BF16),
                pltpu.VMEM((SLOTS, 2 * WIDTH, LANES), F32),
                pltpu.VMEM((SLOTS, 2) + square, F32),
                pltpu.VMEM((SLOTS, 2, 2, 4 * TILE, 128), F32),
                pltpu.VMEM((2, 9, 3, PART, 128), F32),
                pltpu.VMEM((2, 3, 3, 3, PART, 128), F32),
                pltpu.VMEM((2, 3, 3, PART, 128), F32),
                pltpu.VMEM((2 * HALF, 128), F32),
                pltpu.VMEM((HALF, 128), F32),
                pltpu.VMEM((group, share, 128), F32),
                pltpu.VMEM((depth, share, 128), F32),
                pltpu.VMEM((2 * HALF, 128), F32),
                dma((9,)), dma((9,)),
                dma((3,)), dma((3,)), dma((3,)), dma((3,)),
                dma((2, 3)), dma((2, 3)), dma((2, 3)), dma((2, 3)),
                dma, dma,
                dma((owners,)), dma((group,)),
                dma((depth,)), dma((depth,)),
                dma((group,)), dma((owners,)),
                dma((owners,)), dma((owners,)),
            ],
            compiler_params=pltpu.CompilerParams(
                collective_id=0, has_side_effects=True, vmem_limit_bytes=48 * 1024 * 1024
            ),
        )(
            pltpu.with_memory_space_constraint(offsets, pltpu.HBM), counts,
            *[
                pltpu.with_memory_space_constraint(x, pltpu.HBM)
                for x in (object_slices, probe, propagator_phase, measured)
            ],
            *[pltpu.with_memory_space_constraint(jnp.asarray(m), pltpu.HBM) for m in consts],
        )

    return jax.shard_map(
        shards,
        mesh=mesh,
        in_specs=(
            P(None, None, "row", "col"),
            P(),
            P(),
            P("row", "col", None, None, None),
            P("row", "col", None, None),
            P("row", "col"),
        ),
        out_specs=(P(None, None, "row", "col"), P()),
        check_vma=False,
    )
```
